256 devices in a mesh: lon: 16 (over y_lo, z), lat: 8 (over x, core), dep: 2 (over y_hi).
Axes of the slice: x: 4, y: 4 (y_hi: 2, y_lo: 2; y = y_hi * 2 + y_lo), z: 8, core: 2. Of those that a mesh axis runs over, the one named last changes fastest.
Arguments:
- source: float32 [4, 16, 64, 4096], P(None, 'dep', 'lat', 'lon'), may hold values from -48 to 48
- sea_mask: int32 [16, 64, 4096], P('dep', 'lat', 'lon'), may hold values 0 or 1
- classes: int32 [16, 64, 4096], P('dep', 'lat', 'lon'), may hold values from 0 to 7
- kappa_table: float32 [8, 4], replicated, may hold values from 0.05 to 2
- coupling: float32 [4, 4], replicated, may hold values from -0.8 to 0.8
Outputs:
- first_pass: float32 [4, 16, 64, 4096], P(None, 'dep', 'lat', 'lon')
- second_pass: float32 [4, 16, 64, 4096], P(None, 'dep', 'lat', 'lon')
The draws below stay inside these ranges and needn't reach their ends.
All inputs are finite; a program needn't handle non-finite values. No bound on the sum of `sea_mask` on one device may be relied on, other than what follows from the above.
Results may differ from the reference program's by a relative error of at most 0.00011.
Values sent between devices are 32-bit elements; how exact they have to be, the bound alone decides.
No kernel may reach another device: no remote copies, remote signals or barrier semaphores. Data moves between devices by JAX's collectives and lax.ppermute only.
A program may use at most 128 MiB of HBM per device.

```python
import math
import jax
import jax.numpy as jnp

FIELDS = 4
NCLASS = 8
PRE = 3
POST = 3
COARSE = 4
NLON = 4096
NLAT = 64
NDEP = 16


def touch_ends(values, key, least, high):
    extent = values.shape
    place = [jax.random.randint(jax.random.fold_in(key, axis), (), 0, extent[axis]) for axis in range(len(extent))]
    values = values.at[tuple(place)].set(least)
    longest = extent.index(max(extent))
    place[longest] = (place[longest] + 1) % extent[longest]
    return values.at[tuple(place)].set(high)


def block_levels(own_key, shape, shards, low, largest):
    gain, own = 1.0, jax.random.fold_in(own_key, 6)
    for axis_at, blocks in shards:
        draws = jnp.exp(jax.random.uniform(jax.random.fold_in(own, axis_at), (blocks,), jnp.float32, low / len(shards), largest / len(shards)))
        gain = gain * jnp.repeat(draws, shape[axis_at] // blocks).reshape([-1 if axis == axis_at else 1 for axis in range(len(shape))])
    return gain


def gaussian(stream_key, extent, scale, bound, cuts=(), held_as=jnp.bfloat16):
    drawn = jax.random.normal(stream_key, extent, jnp.float32) * scale
    if len(cuts) > 0:
        drawn = block_levels(stream_key, extent, cuts, -0.22, 0.18) * drawn
    return jnp.clip(drawn, min=-bound, max=bound).astype(held_as)


def setup_inputs(seed: int = 0) -> dict:
    key_of = jax.random.split(jax.random.key(seed), 6)
    return {
        "source": gaussian(key_of[0], (FIELDS, NDEP, NLAT, NLON), 8.0, 48.0, ((1, 2), (2, 8), (3, 16)), jnp.float32),
        "sea_mask": touch_ends((jax.random.randint(key_of[1], (NDEP, NLAT, NLON), 0, 5) < 4).astype(jnp.int32), jax.random.fold_in(key_of[1], 1), 0, 1),
        "classes": touch_ends(jax.random.randint(key_of[2], (NDEP, NLAT, NLON), 0, NCLASS), jax.random.fold_in(key_of[2], 1), 0, NCLASS - 1).astype(jnp.int32),
        "kappa_table": jnp.clip(jnp.exp(jax.random.uniform(key_of[3], (NCLASS, FIELDS), jnp.float32, math.log(0.05), math.log(2.0))), 0.05, 2.0),
        "coupling": jnp.clip(jax.random.uniform(key_of[4], (FIELDS, FIELDS), jnp.float32, -0.8, 0.8), -0.8, 0.8),
    }


omega = 0.8


def lookup(classes, table):
    kap = jnp.zeros((table.shape[1],) + classes.shape, jnp.float32)
    for c in range(table.shape[0]):
        kap = kap + jnp.where(classes[None] == c, table[c][:, None, None, None], jnp.float32(0.0))
    return kap


def couple(coupling, u):
    total = coupling[:, 0][:, None, None, None] * u[0][None]
    for g in range(1, u.shape[0]):
        total = total + coupling[:, g][:, None, None, None] * u[g][None]
    return total


def neighbours(v):
    total = jnp.roll(v, 1, 3) + jnp.roll(v, -1, 3)
    padded = jnp.pad(v, ((0, 0), (1, 1), (1, 1), (0, 0)))
    total = total + padded[:, 1:-1, 2:, :] + padded[:, 1:-1, :-2, :]
    total = total + padded[:, 2:, 1:-1, :] + padded[:, :-2, 1:-1, :]
    return total


def apply_op(u, sea, kap, coupling, scale):
    near = neighbours(sea * u)
    return sea * (kap * u + couple(coupling, u) + scale * (6.0 * u - near)) + (1.0 - sea) * u


def diag_of(sea, kap, coupling, scale):
    return sea * (kap + jnp.diagonal(coupling)[:, None, None, None] + 6.0 * scale) + (1.0 - sea)


def sweep(u, b, sea, kap, coupling, scale, diag):
    return u + omega * (b - apply_op(u, sea, kap, coupling, scale)) / diag


def coarsen(x):
    f, d, a, o = x.shape
    return x.reshape(f, d // 2, 2, a // 2, 2, o // 2, 2).mean(axis=(2, 4, 6))


def prolong(e):
    return jnp.repeat(jnp.repeat(jnp.repeat(e, 2, 1), 2, 2), 2, 3)


def vcycle(b, sea, kap, diag, sea_c, kap_c, diag_c, coupling):
    u = jnp.zeros_like(b)
    for step in range(PRE):
        u = sweep(u, b, sea, kap, coupling, 1.0, diag)
    resid = b - apply_op(u, sea, kap, coupling, 1.0)
    rc = sea_c * coarsen(resid)
    e = jnp.zeros_like(rc)
    for step in range(COARSE):
        e = sweep(e, rc, sea_c, kap_c, coupling, 0.25, diag_c)
    u = u + sea * prolong(e)
    for step in range(POST):
        u = sweep(u, b, sea, kap, coupling, 1.0, diag)
    return u


def reference(source, sea_mask, classes, kappa_table, coupling):
    sea = sea_mask.astype(jnp.float32)[None]
    kap = lookup(classes, kappa_table)
    d, a, o = sea_mask.shape
    counts = sea_mask.reshape(d // 2, 2, a // 2, 2, o // 2, 2).sum(axis=(1, 3, 5))
    sea_c = jnp.minimum(counts, 1).astype(jnp.float32)[None]
    kap_c = coarsen(kap)
    diag = diag_of(sea, kap, coupling, 1.0)
    diag_c = diag_of(sea_c, kap_c, coupling, 0.25)
    rhs = sea * source
    first_pass = vcycle(rhs, sea, kap, diag, sea_c, kap_c, diag_c, coupling)
    second_pass = vcycle(first_pass, sea, kap, diag, sea_c, kap_c, diag_c, coupling)
    return first_pass, second_pass
```

```python
import functools

import jax
import jax.numpy as jnp
from jax import lax
from jax.experimental import pallas as pl
from jax.experimental.pallas import tpu as pltpu
from jax.sharding import PartitionSpec as P


FIELDS = 4
CLASSES = 8
OMEGA = 0.8
OWN = 16
HALO = 13
BASE = 14
WIDE = OWN + 2 * BASE
COARSE_WIDE = WIDE // 2
AXES = ("lon", "lat", "dep")
F32 = jnp.float32
VMEM_LIMIT = 48 * 1024 * 1024


def spot(rank):
    return (rank, 0) if rank < 8 else (15 - rank, 1)


def rank_of(lat, dep):
    return lat if dep == 0 else 15 - lat


def device_of(slab):
    block, rank = divmod(slab % 256, 16)
    lat, dep = spot(rank if block % 2 == 0 else 15 - rank)
    return (block * 8 + lat) * 2 + dep


def params():
    return pltpu.CompilerParams(vmem_limit_bytes=VMEM_LIMIT)


def vmem(count):
    return [pl.BlockSpec(memory_space=pltpu.VMEM)] * count


def smem(count):
    return [pl.BlockSpec(memory_space=pltpu.SMEM)] * count


def block_rank(odd, chunk):
    rank = rank_of(chunk // 2, chunk % 2)
    return rank + odd * (15 - 2 * rank)


def pack_kernel(odd_ref, source_ref, sea_ref, classes_ref, out_ref, turned):
    odd = odd_ref[0]
    rows = [source_ref[f].reshape(64, 256) for f in range(FIELDS)]
    rows.append(sea_ref[...].astype(F32).reshape(64, 256))
    rows.append(classes_ref[...].astype(F32).reshape(64, 256))
    for q in range(3):
        pair = jnp.concatenate([rows[2 * q], rows[2 * q + 1]], axis=0)
        for half in range(2):
            turned[q, half * 128 : half * 128 + 128, :] = pair[:, half * 128 : half * 128 + 128].T
    for chunk in range(16):
        at = pl.multiple_of(block_rank(odd, chunk) * 16, 16)
        for q in range(3):
            out_ref[chunk, q * 16 : q * 16 + 16, :] = turned[q, pl.ds(at, 16), :]


def lanes():
    return lax.broadcasted_iota(jnp.int32, (8, 128), 1)


def pick(value, index):
    return jnp.take_along_axis(value, index, axis=1, mode="promise_in_bounds")


def unpack_kernel(in_ref, own_ref, low_ref, high_ref):
    lane = lanes()
    row, depth = lane // 16, lane % 16
    place = (depth % 8) * 8 + row
    upper = depth >= 8
    for o in range(OWN):
        for q in range(3):
            parts = [in_ref[pl.ds(d * 48 + q * 16 + o, 8, stride=96), :] for d in range(2)]
            for half in range(2):
                index = place + 64 * half
                plane = jnp.where(upper, pick(parts[1], index), pick(parts[0], index))
                at = 2 * q + half
                own_ref[o, at] = plane
                if o < HALO:
                    low_ref[o, at] = plane
                if o >= OWN - HALO:
                    high_ref[o - (OWN - HALO), at] = plane


def plane_masks(step):
    lane = lanes()
    row = lax.broadcasted_iota(jnp.int32, (8, 128), 0)
    depth = lane % 16
    return (
        lane < 16 * step,
        row == 7,
        lane >= 128 - 16 * step,
        row == 0,
        jnp.where(depth >= 16 - step, 0.0, 1.0).astype(F32),
        jnp.where(depth < step, 0.0, 1.0).astype(F32),
    )


def plane_near(v, masks, step):
    first, top, last, bottom, keep_up, keep_down = masks
    zero = jnp.zeros_like(v)
    above = jnp.where(first, jnp.where(top, zero, pltpu.roll(v, 7, 0)), v)
    below = jnp.where(last, jnp.where(bottom, zero, pltpu.roll(v, 1, 0)), v)
    total = pltpu.roll(above, 128 - 16 * step, 1) + pltpu.roll(below, 16 * step, 1)
    return total + (pltpu.roll(v, 128 - step, 1) * keep_up + pltpu.roll(v, step, 1) * keep_down)


def stencil(start, stop, u_ref, sea, coupling, masks, step, emit, unroll):
    def load(w):
        u = [u_ref[w, f] for f in range(FIELDS)]
        s = sea(w)
        return u, [s * x for x in u]

    def body(w, carry):
        before, u, v = carry
        u_next, after = load(w + 1)
        for f in range(FIELDS):
            near = (before[f] + after[f]) + plane_near(v[f], masks, step)
            others = [coupling[f][g] * u[g] for g in range(FIELDS) if g != f]
            emit(w, f, u[f], near, others[0] + others[1] + others[2])
        return v, u_next, after

    _, before = load(start - 1)
    u, v = load(start)
    lax.fori_loop(start, stop, body, (before, u, v), unroll=unroll)


def halves(t):
    lane = lanes()
    t = t + jnp.where(lane % 2 == 0, pltpu.roll(t, 127, 1), pltpu.roll(t, 1, 1))
    return t + jnp.where((lane // 16) % 2 == 0, pltpu.roll(t, 112, 1), pltpu.roll(t, 16, 1))


def solve(coupling, fine, coarse, b_sum, u_a, u_b, e_a, e_b, rhs_c):
    gain, size = fine
    gain_c = coarse
    masks, masks_c = plane_masks(1), plane_masks(2)

    def sea(w):
        return gain[w, FIELDS]

    def sea_c(c):
        return gain_c[c, FIELDS]

    def sweep_into(target):
        def emit(w, f, u, near, off):
            target[w, f] = (0.2 * u + b_sum[w, f]) + gain[w, f] * (near - off)

        return emit

    def residual(w, f, u, near, off):
        u_a[w, f] = ((b_sum[w, f] - OMEGA * u) + gain[w, f] * (near - off)) * size[w, f]

    def coarse_into(target):
        def emit(c, f, e, near, off):
            target[c, f] = (0.2 * e + rhs_c[c, f]) + gain_c[c, f] * (0.25 * near - off)

        return emit

    stencil(2, 42, u_a, sea, coupling, masks, 1, sweep_into(u_b), 2)
    stencil(3, 41, u_b, sea, coupling, masks, 1, sweep_into(u_a), 2)

    def residual_b(w, f, u, near, off):
        u_b[w, f] = ((b_sum[w, f] - OMEGA * u) + gain[w, f] * (near - off)) * size[w, f]

    stencil(4, 40, u_a, sea, coupling, masks, 1, residual_b, 2)

    def restrict(c, carry):
        s = sea_c(c)
        for f in range(FIELDS):
            mean = halves(u_b[2 * c, f] + u_b[2 * c + 1, f]) * 0.125
            first = (gain_c[c, f] + (1.0 - s) * OMEGA) * (s * mean)
            rhs_c[c, f] = first
            e_a[c, f] = first
        return carry

    lax.fori_loop(2, 20, restrict, 0, unroll=2)
    stencil(3, 19, e_a, sea_c, coupling, masks_c, 2, coarse_into(e_b), 2)
    stencil(4, 18, e_b, sea_c, coupling, masks_c, 2, coarse_into(e_a), 2)
    stencil(5, 17, e_a, sea_c, coupling, masks_c, 2, coarse_into(e_b), 2)

    def correct(c, carry):
        for f in range(FIELDS):
            e = e_b[c, f]
            for w in (2 * c, 2 * c + 1):
                u_a[w, f] = u_a[w, f] + sea(w) * e
        return carry

    lax.fori_loop(5, 17, correct, 0, unroll=2)
    stencil(12, 32, u_a, sea, coupling, masks, 1, sweep_into(u_b), 2)
    stencil(13, 31, u_b, sea, coupling, masks, 1, sweep_into(u_a), 2)
    stencil(14, 30, u_a, sea, coupling, masks, 1, sweep_into(u_b), 2)


def window(own_ref, low_ref, high_ref, visit):
    for ref, count, first in ((low_ref, HALO, BASE - HALO), (own_ref, OWN, BASE), (high_ref, HALO, BASE + OWN)):

        def body(i, carry, ref=ref, first=first):
            visit(first + i, ref, i)
            return carry

        lax.fori_loop(0, count, body, 0)


def read_coupling(coupling_ref):
    return [[coupling_ref[f, g] for g in range(FIELDS)] for f in range(FIELDS)]


def first_kernel(table_ref, coupling_ref, own_ref, low_ref, high_ref, out_ref, to_low, to_high, gain, size, gain_c,
                 u_a, u_b, e_a, e_b, rhs_c, b_sum):
    coupling = read_coupling(coupling_ref)
    table = [[table_ref[c, f] for f in range(FIELDS)] for c in range(CLASSES)]

    def fine(w, ref, at):
        s = ref[at, 4]
        kind = ref[at, 5]
        gain[w, FIELDS] = s
        hits = [kind == float(c) for c in range(CLASSES)]
        for f in range(FIELDS):
            kappa = jnp.zeros_like(s)
            for c in range(CLASSES):
                kappa = jnp.where(hits[c], table[c][f], kappa)
            diag = s * (kappa + (coupling[f][f] + 6.0)) + (1.0 - s)
            rate = OMEGA / diag
            first = rate * (s * ref[at, f])
            gain[w, f] = s * rate
            size[w, f] = diag * (1.0 / OMEGA)
            b_sum[w, f] = first
            u_a[w, f] = first
            u_b[w, f] = kappa

    window(own_ref, low_ref, high_ref, fine)

    def coarse(c, carry):
        s = jnp.minimum(halves(gain[2 * c, FIELDS] + gain[2 * c + 1, FIELDS]), 1.0)
        gain_c[c, FIELDS] = s
        for f in range(FIELDS):
            kappa = halves(u_b[2 * c, f] + u_b[2 * c + 1, f]) * 0.125
            diag = s * (kappa + (coupling[f][f] + 1.5)) + (1.0 - s)
            gain_c[c, f] = s * (OMEGA / diag)
        return carry

    lax.fori_loop(2, 20, coarse, 0)
    solve(coupling, (gain, size), gain_c, b_sum, u_a, u_b, e_a, e_b, rhs_c)
    for o in range(OWN):
        for f in range(FIELDS):
            plane = u_b[BASE + o, f]
            out_ref[o, f] = plane
            if o < HALO:
                to_low[o, f] = plane
            if o >= OWN - HALO:
                to_high[o - (OWN - HALO), f] = plane


def second_kernel(coupling_ref, own_ref, low_ref, high_ref, gain, size, gain_c, out_ref, u_a, u_b, e_a, e_b, rhs_c, b_sum):
    coupling = read_coupling(coupling_ref)

    def fine(w, ref, at):
        land = (1.0 - gain[w, FIELDS]) * OMEGA
        for f in range(FIELDS):
            first = (gain[w, f] + land) * ref[at, f]
            b_sum[w, f] = first
            u_a[w, f] = first

    window(own_ref, low_ref, high_ref, fine)
    solve(coupling, (gain, size), gain_c, b_sum, u_a, u_b, e_a, e_b, rhs_c)

    lane = lanes()
    place = (lane % 8) * 16 + (lane // 8) % 8
    lower = lane < 64
    for o in range(OWN):
        for k in range(2):
            for q in range(2):
                planes = [own_ref[o, 2 * q + h] if k == 0 else u_b[BASE + o, 2 * q + h] for h in range(2)]
                for d in range(2):
                    index = place + 8 * d
                    rows = jnp.where(lower, pick(planes[0], index), pick(planes[1], index))
                    out_ref[pl.ds(d * 64 + k * 32 + q * 16 + o, 8, stride=128), :] = rows


def finish_kernel(odd_ref, in_ref, first_ref, second_ref, turned):
    odd = odd_ref[0]
    for k, out_ref in enumerate((first_ref, second_ref)):
        for q in range(2):
            for chunk in range(16):
                at = pl.multiple_of(block_rank(odd, chunk) * 16, 16)
                turned[2 * k + q, pl.ds(at, 16), :] = in_ref[chunk, k * 32 + q * 16 : k * 32 + q * 16 + 16, :]
            for half in range(2):
                pair = turned[2 * k + q, half * 128 : half * 128 + 128, :].T
                for h in range(2):
                    out_ref[2 * q + h, :, :, half * 128 : half * 128 + 128] = pair[64 * h : 64 * h + 64].reshape(8, 8, 128)


def planes(count, kinds=FIELDS):
    return jax.ShapeDtypeStruct((count, kinds, 8, 128), F32)


def scratch(count, kinds=FIELDS):
    return pltpu.VMEM((count, kinds, 8, 128), F32)


def per_device(source, sea_mask, classes, kappa_table, coupling):
    odd = (lax.axis_index("lon") % 2).astype(jnp.int32).reshape(1)
    upward = [(device_of(g), device_of(g + 1)) for g in range(256)]
    downward = [(b, a) for a, b in upward]

    sent = pl.pallas_call(
        pack_kernel,
        out_shape=jax.ShapeDtypeStruct((16, 48, 128), F32),
        in_specs=smem(1) + vmem(3),
        out_specs=vmem(1)[0],
        scratch_shapes=[pltpu.VMEM((3, 256, 128), F32)],
        compiler_params=params(),
        name="pack",
    )(odd, source, sea_mask, classes)
    got = lax.all_to_all(sent, ("lat", "dep"), 0, 0, tiled=False)
    own, to_low, to_high = pl.pallas_call(
        unpack_kernel,
        out_shape=(planes(OWN, 6), planes(HALO, 6), planes(HALO, 6)),
        in_specs=vmem(1),
        out_specs=tuple(vmem(3)),
        compiler_params=params(),
        name="unpack",
    )(got.reshape(768, 128))
    low = lax.ppermute(to_high, AXES, upward)
    high = lax.ppermute(to_low, AXES, downward)

    work = [scratch(WIDE), scratch(WIDE), scratch(COARSE_WIDE), scratch(COARSE_WIDE), scratch(COARSE_WIDE), scratch(WIDE)]
    first, to_low, to_high, gain, size, gain_c = pl.pallas_call(
        first_kernel,
        out_shape=(planes(OWN), planes(HALO), planes(HALO), planes(WIDE, 5), planes(WIDE), planes(COARSE_WIDE, 5)),
        in_specs=smem(2) + vmem(3),
        out_specs=tuple(vmem(6)),
        scratch_shapes=work,
        compiler_params=params(),
        name="first",
    )(kappa_table, coupling, own, low, high)
    low = lax.ppermute(to_high, AXES, upward)
    high = lax.ppermute(to_low, AXES, downward)
    sent = pl.pallas_call(
        second_kernel,
        out_shape=jax.ShapeDtypeStruct((1024, 128), F32),
        in_specs=smem(1) + vmem(6),
        out_specs=vmem(1)[0],
        scratch_shapes=work,
        compiler_params=params(),
        name="second",
    )(coupling, first, low, high, gain, size, gain_c)
    got = lax.all_to_all(sent.reshape(16, 64, 128), ("lat", "dep"), 0, 0, tiled=False)
    block = jax.ShapeDtypeStruct((FIELDS, 8, 8, 256), F32)
    return pl.pallas_call(
        finish_kernel,
        out_shape=(block, block),
        in_specs=smem(1) + vmem(1),
        out_specs=tuple(vmem(2)),
        scratch_shapes=[pltpu.VMEM((4, 256, 128), F32)],
        compiler_params=params(),
        name="finish",
    )(odd, got)


def solution(mesh):
    return jax.shard_map(
        per_device,
        mesh=mesh,
        in_specs=(
            P(None, "dep", "lat", "lon"),
            P("dep", "lat", "lon"),
            P("dep", "lat", "lon"),
            P(),
            P(),
        ),
        out_specs=(P(None, "dep", "lat", "lon"), P(None, "dep", "lat", "lon")),
        check_vma=False,
    )
```

```python
import functools

import jax
import jax.numpy as jnp
from jax import lax
from jax.experimental import pallas as pl
from jax.experimental.pallas import tpu as pltpu
from jax.sharding import PartitionSpec as P


FIELDS = 4
CLASSES = 8
OMEGA = 0.8
OWN = 16
HALO = 13
BASE = 14
WIDE = OWN + 2 * BASE
COARSE_WIDE = WIDE // 2
UNROLL = (6, 2, 4, 6)
AXES = ("lon", "lat", "dep")
F32 = jnp.float32
VMEM_LIMIT = 48 * 1024 * 1024


def spot(rank):
    return (rank, 0) if rank < 8 else (15 - rank, 1)


def rank_of(lat, dep):
    return lat if dep == 0 else 15 - lat


def device_of(slab):
    block, rank = divmod(slab % 256, 16)
    lat, dep = spot(rank if block % 2 == 0 else 15 - rank)
    return (block * 8 + lat) * 2 + dep


def params():
    return pltpu.CompilerParams(vmem_limit_bytes=VMEM_LIMIT)


def vmem(count):
    return [pl.BlockSpec(memory_space=pltpu.VMEM)] * count


def smem(count):
    return [pl.BlockSpec(memory_space=pltpu.SMEM)] * count


def block_rank(odd, chunk):
    rank = rank_of(chunk // 2, chunk % 2)
    return rank + odd * (15 - 2 * rank)


def pack_kernel(odd_ref, source_ref, sea_ref, classes_ref, out_ref, turned):
    odd = odd_ref[0]
    rows = [source_ref[f].reshape(64, 256) for f in range(FIELDS)]
    rows.append(sea_ref[...].astype(F32).reshape(64, 256))
    rows.append(classes_ref[...].astype(F32).reshape(64, 256))
    for q in range(3):
        pair = jnp.concatenate([rows[2 * q], rows[2 * q + 1]], axis=0)
        for half in range(2):
            turned[q, half * 128 : half * 128 + 128, :] = pair[:, half * 128 : half * 128 + 128].T
    for chunk in range(16):
        at = pl.multiple_of(block_rank(odd, chunk) * 16, 16)
        for q in range(3):
            out_ref[chunk, q * 16 : q * 16 + 16, :] = turned[q, pl.ds(at, 16), :]


def lanes():
    return lax.broadcasted_iota(jnp.int32, (8, 128), 1)


def pick(value, index):
    return jnp.take_along_axis(value, index, axis=1, mode="promise_in_bounds")


def unpack_kernel(in_ref, own_ref, low_ref, high_ref):
    lane = lanes()
    row, depth = lane // 16, lane % 16
    place = (depth % 8) * 8 + row
    upper = depth >= 8
    for o in range(OWN):
        for q in range(3):
            parts = [in_ref[pl.ds(d * 48 + q * 16 + o, 8, stride=96), :] for d in range(2)]
            for half in range(2):
                index = place + 64 * half
                plane = jnp.where(upper, pick(parts[1], index), pick(parts[0], index))
                at = 2 * q + half
                own_ref[o, at] = plane
                if o < HALO:
                    low_ref[o, at] = plane
                if o >= OWN - HALO:
                    high_ref[o - (OWN - HALO), at] = plane


def plane_masks(step):
    lane = lanes()
    row = lax.broadcasted_iota(jnp.int32, (8, 128), 0)
    depth = lane % 16
    return (
        lane < 16 * step,
        row == 7,
        lane >= 128 - 16 * step,
        row == 0,
        jnp.where(depth >= 16 - step, 0.0, 1.0).astype(F32),
        jnp.where(depth < step, 0.0, 1.0).astype(F32),
    )


def plane_near(v, masks, step):
    first, top, last, bottom, keep_up, keep_down = masks
    zero = jnp.zeros_like(v)
    above = jnp.where(first, jnp.where(top, zero, pltpu.roll(v, 7, 0)), v)
    below = jnp.where(last, jnp.where(bottom, zero, pltpu.roll(v, 1, 0)), v)
    total = pltpu.roll(above, 128 - 16 * step, 1) + pltpu.roll(below, 16 * step, 1)
    return total + (pltpu.roll(v, 128 - step, 1) * keep_up + pltpu.roll(v, step, 1) * keep_down)


def stencil(start, stop, u_ref, sea, coupling, masks, step, emit):
    def load(w):
        u = [u_ref[w, f] for f in range(FIELDS)]
        s = sea(w)
        return u, [s * x for x in u]

    _, before = load(start - 1)
    u, v = load(start)
    for w in range(start, stop):
        u_next, after = load(w + 1)
        for f in range(FIELDS):
            near = (before[f] + after[f]) + plane_near(v[f], masks, step)
            others = [coupling[f][g] * u[g] for g in range(FIELDS) if g != f]
            emit(w, f, u[f], near, others[0] + others[1] + others[2])
        before, u, v = v, u_next, after


def halves(t):
    lane = lanes()
    t = t + jnp.where(lane % 2 == 0, pltpu.roll(t, 127, 1), pltpu.roll(t, 1, 1))
    return t + jnp.where((lane // 16) % 2 == 0, pltpu.roll(t, 112, 1), pltpu.roll(t, 16, 1))


def solve(coupling, fine, coarse, b_sum, u_a, u_b, e_a, e_b, rhs_c):
    gain, size = fine
    gain_c = coarse
    masks, masks_c = plane_masks(1), plane_masks(2)

    def sea(w):
        return gain[w, FIELDS]

    def sea_c(c):
        return gain_c[c, FIELDS]

    def sweep_into(target):
        def emit(w, f, u, near, off):
            target[w, f] = (0.2 * u + b_sum[w, f]) + gain[w, f] * (near - off)

        return emit

    def coarse_into(target):
        def emit(c, f, e, near, off):
            target[c, f] = (0.2 * e + rhs_c[c, f]) + gain_c[c, f] * (0.25 * near - off)

        return emit

    stencil(2, 42, u_a, sea, coupling, masks, 1, sweep_into(u_b))
    stencil(3, 41, u_b, sea, coupling, masks, 1, sweep_into(u_a))

    def residual(w, f, u, near, off):
        u_b[w, f] = ((b_sum[w, f] - OMEGA * u) + gain[w, f] * (near - off)) * size[w, f]

    stencil(4, 40, u_a, sea, coupling, masks, 1, residual)

    def restrict(c, carry):
        s = sea_c(c)
        for f in range(FIELDS):
            mean = halves(u_b[2 * c, f] + u_b[2 * c + 1, f]) * 0.125
            first = (gain_c[c, f] + (1.0 - s) * OMEGA) * (s * mean)
            rhs_c[c, f] = first
            e_a[c, f] = first
        return carry

    lax.fori_loop(2, 20, restrict, 0, unroll=UNROLL[0])
    stencil(3, 19, e_a, sea_c, coupling, masks_c, 2, coarse_into(e_b))
    stencil(4, 18, e_b, sea_c, coupling, masks_c, 2, coarse_into(e_a))
    stencil(5, 17, e_a, sea_c, coupling, masks_c, 2, coarse_into(e_b))

    def correct(c, carry):
        for f in range(FIELDS):
            e = e_b[c, f]
            for w in (2 * c, 2 * c + 1):
                u_a[w, f] = u_a[w, f] + sea(w) * e
        return carry

    lax.fori_loop(5, 17, correct, 0, unroll=UNROLL[1])
    stencil(12, 32, u_a, sea, coupling, masks, 1, sweep_into(u_b))
    stencil(13, 31, u_b, sea, coupling, masks, 1, sweep_into(u_a))
    stencil(14, 30, u_a, sea, coupling, masks, 1, sweep_into(u_b))


def window(own_ref, low_ref, high_ref, visit):
    for ref, count, first in ((low_ref, HALO, BASE - HALO), (own_ref, OWN, BASE), (high_ref, HALO, BASE + OWN)):

        def body(i, carry, ref=ref, first=first):
            visit(first + i, ref, i)
            return carry

        lax.fori_loop(0, count, body, 0, unroll=UNROLL[2])


def read_coupling(coupling_ref):
    return [[coupling_ref[f, g] for g in range(FIELDS)] for f in range(FIELDS)]


def first_kernel(table_ref, coupling_ref, own_ref, low_ref, high_ref, out_ref, to_low, to_high, gain, size, gain_c,
                 u_a, u_b, e_a, e_b, rhs_c, b_sum):
    coupling = read_coupling(coupling_ref)
    table = [[table_ref[c, f] for f in range(FIELDS)] for c in range(CLASSES)]

    def fine(w, ref, at):
        s = ref[at, 4]
        kind = ref[at, 5]
        gain[w, FIELDS] = s
        hits = [kind == float(c) for c in range(CLASSES)]
        for f in range(FIELDS):
            kappa = jnp.zeros_like(s)
            for c in range(CLASSES):
                kappa = jnp.where(hits[c], table[c][f], kappa)
            diag = s * (kappa + (coupling[f][f] + 6.0)) + (1.0 - s)
            rate = OMEGA / diag
            first = rate * (s * ref[at, f])
            gain[w, f] = s * rate
            size[w, f] = diag * (1.0 / OMEGA)
            b_sum[w, f] = first
            u_a[w, f] = first
            u_b[w, f] = kappa

    window(own_ref, low_ref, high_ref, fine)

    def coarse(c, carry):
        s = jnp.minimum(halves(gain[2 * c, FIELDS] + gain[2 * c + 1, FIELDS]), 1.0)
        gain_c[c, FIELDS] = s
        for f in range(FIELDS):
            kappa = halves(u_b[2 * c, f] + u_b[2 * c + 1, f]) * 0.125
            diag = s * (kappa + (coupling[f][f] + 1.5)) + (1.0 - s)
            gain_c[c, f] = s * (OMEGA / diag)
        return carry

    lax.fori_loop(2, 20, coarse, 0, unroll=UNROLL[3])
    solve(coupling, (gain, size), gain_c, b_sum, u_a, u_b, e_a, e_b, rhs_c)
    for o in range(OWN):
        for f in range(FIELDS):
            plane = u_b[BASE + o, f]
            out_ref[o, f] = plane
            if o < HALO:
                to_low[o, f] = plane
            if o >= OWN - HALO:
                to_high[o - (OWN - HALO), f] = plane


def second_kernel(coupling_ref, own_ref, low_ref, high_ref, gain, size, gain_c, out_ref, u_a, u_b, e_a, e_b, rhs_c, b_sum):
    coupling = read_coupling(coupling_ref)

    def fine(w, ref, at):
        land = (1.0 - gain[w, FIELDS]) * OMEGA
        for f in range(FIELDS):
            first = (gain[w, f] + land) * ref[at, f]
            b_sum[w, f] = first
            u_a[w, f] = first

    window(own_ref, low_ref, high_ref, fine)
    solve(coupling, (gain, size), gain_c, b_sum, u_a, u_b, e_a, e_b, rhs_c)

    lane = lanes()
    place = (lane % 8) * 16 + (lane // 8) % 8
    lower = lane < 64
    for o in range(OWN):
        for k in range(2):
            for q in range(2):
                planes = [own_ref[o, 2 * q + h] if k == 0 else u_b[BASE + o, 2 * q + h] for h in range(2)]
                for d in range(2):
                    index = place + 8 * d
                    rows = jnp.where(lower, pick(planes[0], index), pick(planes[1], index))
                    out_ref[pl.ds(d * 64 + k * 32 + q * 16 + o, 8, stride=128), :] = rows


def finish_kernel(odd_ref, in_ref, first_ref, second_ref, turned):
    odd = odd_ref[0]
    for k, out_ref in enumerate((first_ref, second_ref)):
        for q in range(2):
            for chunk in range(16):
                at = pl.multiple_of(block_rank(odd, chunk) * 16, 16)
                turned[2 * k + q, pl.ds(at, 16), :] = in_ref[chunk, k * 32 + q * 16 : k * 32 + q * 16 + 16, :]
            for half in range(2):
                pair = turned[2 * k + q, half * 128 : half * 128 + 128, :].T
                for h in range(2):
                    out_ref[2 * q + h, :, :, half * 128 : half * 128 + 128] = pair[64 * h : 64 * h + 64].reshape(8, 8, 128)


def planes(count, kinds=FIELDS):
    return jax.ShapeDtypeStruct((count, kinds, 8, 128), F32)


def scratch(count, kinds=FIELDS):
    return pltpu.VMEM((count, kinds, 8, 128), F32)


def per_device(source, sea_mask, classes, kappa_table, coupling):
    odd = (lax.axis_index("lon") % 2).astype(jnp.int32).reshape(1)
    upward = [(device_of(g), device_of(g + 1)) for g in range(256)]
    downward = [(b, a) for a, b in upward]

    sent = pl.pallas_call(
        pack_kernel,
        out_shape=jax.ShapeDtypeStruct((16, 48, 128), F32),
        in_specs=smem(1) + vmem(3),
        out_specs=vmem(1)[0],
        scratch_shapes=[pltpu.VMEM((3, 256, 128), F32)],
        compiler_params=params(),
        name="pack",
    )(odd, source, sea_mask, classes)
    got = lax.all_to_all(sent, ("lat", "dep"), 0, 0, tiled=False)
    own, to_low, to_high = pl.pallas_call(
        unpack_kernel,
        out_shape=(planes(OWN, 6), planes(HALO, 6), planes(HALO, 6)),
        in_specs=vmem(1),
        out_specs=tuple(vmem(3)),
        compiler_params=params(),
        name="unpack",
    )(got.reshape(768, 128))
    low = lax.ppermute(to_high, AXES, upward)
    high = lax.ppermute(to_low, AXES, downward)

    work = [scratch(WIDE), scratch(WIDE), scratch(COARSE_WIDE), scratch(COARSE_WIDE), scratch(COARSE_WIDE), scratch(WIDE)]
    first, to_low, to_high, gain, size, gain_c = pl.pallas_call(
        first_kernel,
        out_shape=(planes(OWN), planes(HALO), planes(HALO), planes(WIDE, 5), planes(WIDE), planes(COARSE_WIDE, 5)),
        in_specs=smem(2) + vmem(3),
        out_specs=tuple(vmem(6)),
        scratch_shapes=work,
        compiler_params=params(),
        name="first",
    )(kappa_table, coupling, own, low, high)
    low = lax.ppermute(to_high, AXES, upward)
    high = lax.ppermute(to_low, AXES, downward)
    sent = pl.pallas_call(
        second_kernel,
        out_shape=jax.ShapeDtypeStruct((1024, 128), F32),
        in_specs=smem(1) + vmem(6),
        out_specs=vmem(1)[0],
        scratch_shapes=work,
        compiler_params=params(),
        name="second",
    )(coupling, first, low, high, gain, size, gain_c)
    got = lax.all_to_all(sent.reshape(16, 64, 128), ("lat", "dep"), 0, 0, tiled=False)
    block = jax.ShapeDtypeStruct((FIELDS, 8, 8, 256), F32)
    return pl.pallas_call(
        finish_kernel,
        out_shape=(block, block),
        in_specs=smem(1) + vmem(1),
        out_specs=tuple(vmem(2)),
        scratch_shapes=[pltpu.VMEM((4, 256, 128), F32)],
        compiler_params=params(),
        name="finish",
    )(odd, got)


def solution(mesh):
    return jax.shard_map(
        per_device,
        mesh=mesh,
        in_specs=(
            P(None, "dep", "lat", "lon"),
            P("dep", "lat", "lon"),
            P("dep", "lat", "lon"),
            P(),
            P(),
        ),
        out_specs=(P(None, "dep", "lat", "lon"), P(None, "dep", "lat", "lon")),
        check_vma=False,
    )
```

```python
import functools

import jax
import jax.numpy as jnp
from jax import lax
from jax.experimental import pallas as pl
from jax.experimental.pallas import tpu as pltpu
from jax.sharding import PartitionSpec as P


FIELDS = 4
CLASSES = 8
OMEGA = 0.8
OWN = 16
HALO = 13
BASE = 14
WIDE = OWN + 2 * BASE
COARSE_WIDE = WIDE // 2
UNROLL = (6, 2, 4, 5, 4)
AXES = ("lon", "lat", "dep")
F32 = jnp.float32
VMEM_LIMIT = 48 * 1024 * 1024


PATHS = (
    ((3, 1), (2, 1), (1, 1), (0, 1), (0, 0), (1, 0), (2, 0), (3, 0)),
    ((3, 1), (2, 1), (1, 1), (0, 1), (0, 0), (1, 0), (2, 0), (3, 0)),
)


def spots(path):
    return [(2 * x + core, dep) for x, dep in path for core in ((0, 1) if dep else (1, 0))]


PLACES = [spots(path) for path in PATHS]


def device_of(slab):
    block, rank = divmod(slab % 256, 16)
    lat, dep = PLACES[block // 8][rank if block % 2 == 0 else 15 - rank]
    return (block * 8 + lat) * 2 + dep


def params():
    return pltpu.CompilerParams(vmem_limit_bytes=VMEM_LIMIT)


def vmem(count):
    return [pl.BlockSpec(memory_space=pltpu.VMEM)] * count


def smem(count):
    return [pl.BlockSpec(memory_space=pltpu.SMEM)] * count


def block_rank(block, chunk):
    low, high = (places.index((chunk // 2, chunk % 2)) for places in PLACES)
    rank = low if low == high else jnp.where(block < 8, low, high)
    odd = lax.rem(block, 2)
    return rank + odd * (15 - 2 * rank)


def pack_kernel(block_ref, rows_ref, out_ref, turned):
    block = block_ref[0]
    for q in range(3):
        for half in range(2):
            tile = rows_ref[128 * q : 128 * q + 128, half * 128 : half * 128 + 128]
            turned[q, half * 128 : half * 128 + 128, :] = tile.T
    for chunk in range(16):
        at = pl.multiple_of(block_rank(block, chunk) * 16, 16)
        for q in range(3):
            out_ref[chunk, q * 16 : q * 16 + 16, :] = turned[q, pl.ds(at, 16), :]


def lanes():
    return lax.broadcasted_iota(jnp.int32, (8, 128), 1)


def pick(value, index):
    return jnp.take_along_axis(value, index, axis=1, mode="promise_in_bounds")


def unpack_kernel(in_ref, own_ref, low_ref, high_ref):
    lane = lanes()
    row, depth = lane // 16, lane % 16
    place = (depth % 8) * 8 + row
    upper = depth >= 8
    for o in range(OWN):
        for q in range(3):
            parts = [in_ref[pl.ds(d * 48 + q * 16 + o, 8, stride=96), :] for d in range(2)]
            for half in range(2):
                index = place + 64 * half
                plane = jnp.where(upper, pick(parts[1], index), pick(parts[0], index))
                at = 2 * q + half
                own_ref[o, at] = plane
                if o < HALO:
                    low_ref[o, at] = plane
                if o >= OWN - HALO:
                    high_ref[o - (OWN - HALO), at] = plane


def plane_masks(step):
    lane = lanes()
    row = lax.broadcasted_iota(jnp.int32, (8, 128), 0)
    depth = lane % 16
    return (
        lane < 16 * step,
        row == 7,
        lane >= 128 - 16 * step,
        row == 0,
        jnp.where(depth >= 16 - step, 0.0, 1.0).astype(F32),
        jnp.where(depth < step, 0.0, 1.0).astype(F32),
    )


def plane_near(v, masks, step):
    first, top, last, bottom, keep_up, keep_down = masks
    zero = jnp.zeros_like(v)
    above = jnp.where(first, jnp.where(top, zero, pltpu.roll(v, 7, 0)), v)
    below = jnp.where(last, jnp.where(bottom, zero, pltpu.roll(v, 1, 0)), v)
    total = pltpu.roll(above, 128 - 16 * step, 1) + pltpu.roll(below, 16 * step, 1)
    return total + (pltpu.roll(v, 128 - step, 1) * keep_up + pltpu.roll(v, step, 1) * keep_down)


def stencil(start, stop, u_ref, sea, coupling, masks, step, emit):
    def load(w):
        u = [u_ref[w, f] for f in range(FIELDS)]
        s = sea(w)
        return u, [s * x for x in u]

    _, before = load(start - 1)
    u, v = load(start)
    for w in range(start, stop):
        u_next, after = load(w + 1)
        for f in range(FIELDS):
            near = (before[f] + after[f]) + plane_near(v[f], masks, step)
            others = [coupling[f][g] * u[g] for g in range(FIELDS) if g != f]
            emit(w, f, u[f], near, others[0] + others[1] + others[2])
        before, u, v = v, u_next, after


def halves(t):
    lane = lanes()
    t = t + jnp.where(lane % 2 == 0, pltpu.roll(t, 127, 1), pltpu.roll(t, 1, 1))
    return t + jnp.where((lane // 16) % 2 == 0, pltpu.roll(t, 112, 1), pltpu.roll(t, 16, 1))


def fine_passes(coupling, coeffs, u_a, u_b):
    gain, size, b_sum = coeffs
    masks = plane_masks(1)

    def sea(w):
        return gain[w, FIELDS]

    def sweep_into(target):
        def emit(w, f, u, near, off):
            target[w, f] = (0.2 * u + b_sum[w, f]) + gain[w, f] * (near - off)

        return emit

    def residual(w, f, u, near, off):
        u_b[w, f] = ((b_sum[w, f] - OMEGA * u) + gain[w, f] * (near - off)) * size[w, f]

    def a_to_b(start, stop):
        stencil(start, stop, u_a, sea, coupling, masks, 1, sweep_into(u_b))

    def b_to_a(start, stop):
        stencil(start, stop, u_b, sea, coupling, masks, 1, sweep_into(u_a))

    def rest(start, stop):
        stencil(start, stop, u_a, sea, coupling, masks, 1, residual)

    return a_to_b, b_to_a, rest


def inner_passes(coupling, coeffs, u_a, u_b):
    for turn, one in enumerate(fine_passes(coupling, coeffs, u_a, u_b)):
        one(BASE + 1 + turn, BASE + OWN - 1 - turn)


def solve(coupling, coeffs, gain_c, u_a, u_b, e_a, e_b, rhs_c):
    gain = coeffs[0]
    passes = fine_passes(coupling, coeffs, u_a, u_b)
    for turn, one in enumerate(passes):
        one(BASE - HALO + 1 + turn, BASE + 1 + turn)
        one(BASE + OWN - 1 - turn, BASE + OWN + HALO - 1 - turn)

    masks_c = plane_masks(2)

    def sea_c(c):
        return gain_c[c, FIELDS]

    def coarse_into(target):
        def emit(c, f, e, near, off):
            target[c, f] = (0.2 * e + rhs_c[c, f]) + gain_c[c, f] * (0.25 * near - off)

        return emit

    def restrict(c, carry):
        s = sea_c(c)
        for f in range(FIELDS):
            mean = halves(u_b[2 * c, f] + u_b[2 * c + 1, f]) * 0.125
            first = (gain_c[c, f] + (1.0 - s) * OMEGA) * (s * mean)
            rhs_c[c, f] = first
            e_a[c, f] = first
        return carry

    lax.fori_loop(2, 20, restrict, 0, unroll=UNROLL[0])
    stencil(3, 19, e_a, sea_c, coupling, masks_c, 2, coarse_into(e_b))
    stencil(4, 18, e_b, sea_c, coupling, masks_c, 2, coarse_into(e_a))
    stencil(5, 17, e_a, sea_c, coupling, masks_c, 2, coarse_into(e_b))

    def correct(c, carry):
        for f in range(FIELDS):
            e = e_b[c, f]
            for w in (2 * c, 2 * c + 1):
                u_a[w, f] = u_a[w, f] + gain[w, FIELDS] * e
        return carry

    lax.fori_loop(5, 17, correct, 0, unroll=UNROLL[1])
    passes[0](12, 32)
    passes[1](13, 31)
    passes[0](14, 30)


def each_plane(ref, count, first, visit, unroll):
    def body(i, carry):
        visit(first + i, ref, i)
        return carry

    lax.fori_loop(0, count, body, 0, unroll=unroll)


def read_coupling(coupling_ref):
    return [[coupling_ref[f, g] for g in range(FIELDS)] for f in range(FIELDS)]


def fine_coefficients(table, coupling, coeffs, u_a, kappas):
    gain, size, b_sum = coeffs

    def visit(w, ref, at):
        s = ref[at, 4]
        kind = ref[at, 5]
        gain[w, FIELDS] = s
        hits = [kind == float(c) for c in range(CLASSES)]
        for f in range(FIELDS):
            kappa = jnp.zeros_like(s)
            for c in range(CLASSES):
                kappa = jnp.where(hits[c], table[c][f], kappa)
            diag = s * (kappa + (coupling[f][f] + 6.0)) + (1.0 - s)
            rate = OMEGA / diag
            first = rate * (s * ref[at, f])
            gain[w, f] = s * rate
            size[w, f] = diag * (1.0 / OMEGA)
            b_sum[w, f] = first
            u_a[w, f] = first
            kappas[w, f] = kappa

    return visit


def coarse_coefficients(coupling, gain, gain_c, kappas):
    def visit(c, carry):
        s = jnp.minimum(halves(gain[2 * c, FIELDS] + gain[2 * c + 1, FIELDS]), 1.0)
        gain_c[c, FIELDS] = s
        for f in range(FIELDS):
            kappa = halves(kappas[2 * c, f] + kappas[2 * c + 1, f]) * 0.125
            diag = s * (kappa + (coupling[f][f] + 1.5)) + (1.0 - s)
            gain_c[c, f] = s * (OMEGA / diag)
        return carry

    return visit


def inner_first_kernel(table_ref, coupling_ref, own_ref, gain, size, b_sum, gain_c, u_a, u_b):
    coupling = read_coupling(coupling_ref)
    table = [[table_ref[c, f] for f in range(FIELDS)] for c in range(CLASSES)]
    coeffs = (gain, size, b_sum)
    each_plane(own_ref, OWN, BASE, fine_coefficients(table, coupling, coeffs, u_a, u_b), UNROLL[2])
    lax.fori_loop(7, 15, coarse_coefficients(coupling, gain, gain_c, u_b), 0, unroll=UNROLL[4])
    inner_passes(coupling, coeffs, u_a, u_b)


def first_kernel(table_ref, coupling_ref, low_ref, high_ref, *refs):
    gain, size, b_sum, gain_c, u_a, u_b, out_ref, to_low, to_high, e_a, e_b, rhs_c, kappas = refs[6:]
    coupling = read_coupling(coupling_ref)
    table = [[table_ref[c, f] for f in range(FIELDS)] for c in range(CLASSES)]
    coeffs = (gain, size, b_sum)
    visit = fine_coefficients(table, coupling, coeffs, u_a, kappas)
    each_plane(low_ref, HALO, BASE - HALO, visit, UNROLL[2])
    each_plane(high_ref, HALO, BASE + OWN, visit, UNROLL[2])
    visit = coarse_coefficients(coupling, gain, gain_c, kappas)
    lax.fori_loop(0, 10, lambda i, carry: visit(i + jnp.where(i < 5, 2, 10), carry), 0, unroll=UNROLL[3])
    solve(coupling, coeffs, gain_c, u_a, u_b, e_a, e_b, rhs_c)
    out_ref[...] = u_b[BASE : BASE + OWN]
    to_low[...] = u_b[BASE : BASE + HALO]
    to_high[...] = u_b[BASE + OWN - HALO : BASE + OWN]


def second_start(coeffs, u_a):
    gain, _, b_sum = coeffs

    def visit(w, ref, at):
        land = (1.0 - gain[w, FIELDS]) * OMEGA
        for f in range(FIELDS):
            first = (gain[w, f] + land) * ref[at, f]
            b_sum[w, f] = first
            u_a[w, f] = first

    return visit


def inner_second_kernel(coupling_ref, own_ref, gain, size, b_sum, u_a, u_b):
    coeffs = (gain, size, b_sum)
    each_plane(own_ref, OWN, BASE, second_start(coeffs, u_a), UNROLL[2])
    inner_passes(read_coupling(coupling_ref), coeffs, u_a, u_b)


def second_kernel(coupling_ref, own_ref, low_ref, high_ref, gain, size, gain_c, *refs):
    b_sum, u_a, u_b, out_ref, e_a, e_b, rhs_c = refs[3:]
    coupling = read_coupling(coupling_ref)
    coeffs = (gain, size, b_sum)
    each_plane(low_ref, HALO, BASE - HALO, second_start(coeffs, u_a), UNROLL[2])
    each_plane(high_ref, HALO, BASE + OWN, second_start(coeffs, u_a), UNROLL[2])
    solve(coupling, coeffs, gain_c, u_a, u_b, e_a, e_b, rhs_c)

    lane = lanes()
    place = (lane % 8) * 16 + (lane // 8) % 8
    lower = lane < 64
    for o in range(OWN):
        for k in range(2):
            for q in range(2):
                planes = [own_ref[o, 2 * q + h] if k == 0 else u_b[BASE + o, 2 * q + h] for h in range(2)]
                for d in range(2):
                    index = place + 8 * d
                    rows = jnp.where(lower, pick(planes[0], index), pick(planes[1], index))
                    out_ref[pl.ds(d * 64 + k * 32 + q * 16 + o, 8, stride=128), :] = rows


def finish_kernel(block_ref, in_ref, first_ref, second_ref, turned):
    block = block_ref[0]
    for k, out_ref in enumerate((first_ref, second_ref)):
        for q in range(2):
            for chunk in range(16):
                at = pl.multiple_of(block_rank(block, chunk) * 16, 16)
                turned[2 * k + q, pl.ds(at, 16), :] = in_ref[chunk, k * 32 + q * 16 : k * 32 + q * 16 + 16, :]
            for half in range(2):
                pair = turned[2 * k + q, half * 128 : half * 128 + 128, :].T
                for h in range(2):
                    out_ref[2 * q + h, :, :, half * 128 : half * 128 + 128] = pair[64 * h : 64 * h + 64].reshape(8, 8, 128)


def planes(count, kinds=FIELDS):
    return jax.ShapeDtypeStruct((count, kinds, 8, 128), F32)


def scratch(count, kinds=FIELDS):
    return pltpu.VMEM((count, kinds, 8, 128), F32)


def per_device(source, sea_mask, classes, kappa_table, coupling):
    block = lax.axis_index("lon").astype(jnp.int32).reshape(1)
    upward = [(device_of(g), device_of(g + 1)) for g in range(256)]
    downward = [(b, a) for a, b in upward]

    sent = pl.pallas_call(
        pack_kernel,
        out_shape=jax.ShapeDtypeStruct((16, 48, 128), F32),
        in_specs=smem(1) + vmem(1),
        out_specs=vmem(1)[0],
        scratch_shapes=[pltpu.VMEM((3, 256, 128), F32)],
        compiler_params=params(),
        name="pack",
    )(block, jnp.concatenate([x.astype(F32).reshape(-1, 256) for x in (source, sea_mask, classes)]))
    got = lax.all_to_all(sent, ("lat", "dep"), 0, 0, tiled=False)
    own, to_low, to_high = pl.pallas_call(
        unpack_kernel,
        out_shape=(planes(OWN, 6), planes(HALO, 6), planes(HALO, 6)),
        in_specs=vmem(1),
        out_specs=tuple(vmem(3)),
        compiler_params=params(),
        name="unpack",
    )(got.reshape(768, 128))
    low = lax.ppermute(to_high, AXES, upward)
    high = lax.ppermute(to_low, AXES, downward)

    cost = pl.CostEstimate(flops=40_000_000, bytes_accessed=8_000_000, transcendentals=0)
    coarse = [scratch(COARSE_WIDE)] * 3
    state = (planes(WIDE, 5), planes(WIDE), planes(WIDE), planes(COARSE_WIDE, 5), planes(WIDE), planes(WIDE))
    state = pl.pallas_call(
        inner_first_kernel,
        out_shape=state,
        in_specs=smem(2) + vmem(1),
        out_specs=tuple(vmem(6)),
        compiler_params=params(),
        cost_estimate=cost,
        name="inner_first",
    )(kappa_table, coupling, own)
    gain, size, _, gain_c, _, _, first, to_low, to_high = pl.pallas_call(
        first_kernel,
        out_shape=tuple(state) + (planes(OWN), planes(HALO), planes(HALO)),
        in_specs=smem(2) + vmem(8),
        out_specs=tuple(vmem(9)),
        scratch_shapes=coarse + [scratch(WIDE)],
        input_output_aliases={4 + i: i for i in range(6)},
        compiler_params=params(),
        cost_estimate=cost,
        name="first",
    )(kappa_table, coupling, low, high, *state)
    low = lax.ppermute(to_high, AXES, upward)
    high = lax.ppermute(to_low, AXES, downward)
    state = pl.pallas_call(
        inner_second_kernel,
        out_shape=(planes(WIDE), planes(WIDE), planes(WIDE)),
        in_specs=smem(1) + vmem(3),
        out_specs=tuple(vmem(3)),
        compiler_params=params(),
        cost_estimate=cost,
        name="inner_second",
    )(coupling, first, gain, size)
    _, _, _, sent = pl.pallas_call(
        second_kernel,
        out_shape=tuple(state) + (jax.ShapeDtypeStruct((1024, 128), F32),),
        in_specs=smem(1) + vmem(9),
        out_specs=tuple(vmem(4)),
        scratch_shapes=coarse,
        input_output_aliases={7 + i: i for i in range(3)},
        compiler_params=params(),
        cost_estimate=cost,
        name="second",
    )(coupling, first, low, high, gain, size, gain_c, *state)
    got = lax.all_to_all(sent.reshape(16, 64, 128), ("lat", "dep"), 0, 0, tiled=False)
    out = jax.ShapeDtypeStruct((FIELDS, 8, 8, 256), F32)
    return pl.pallas_call(
        finish_kernel,
        out_shape=(out, out),
        in_specs=smem(1) + vmem(1),
        out_specs=tuple(vmem(2)),
        scratch_shapes=[pltpu.VMEM((4, 256, 128), F32)],
        compiler_params=params(),
        name="finish",
    )(block, got)


def solution(mesh):
    return jax.shard_map(
        per_device,
        mesh=mesh,
        in_specs=(
            P(None, "dep", "lat", "lon"),
            P("dep", "lat", "lon"),
            P("dep", "lat", "lon"),
            P(),
            P(),
        ),
        out_specs=(P(None, "dep", "lat", "lon"), P(None, "dep", "lat", "lon")),
        check_vma=False,
    )
```

```python
import functools

import jax
import jax.numpy as jnp
from jax import lax
from jax.experimental import pallas as pl
from jax.experimental.pallas import tpu as pltpu
from jax.sharding import PartitionSpec as P


FIELDS = 4
CLASSES = 8
OMEGA = 0.8
OWN = 16
HALO = 13
BASE = 14
WIDE = OWN + 2 * BASE
COARSE_WIDE = WIDE // 2
UNROLL = (6, 2, 4, 4)
AXES = ("lon", "lat", "dep")
F32 = jnp.float32
VMEM_LIMIT = 48 * 1024 * 1024


PATHS = (
    ((3, 1), (2, 1), (1, 1), (0, 1), (0, 0), (1, 0), (2, 0), (3, 0)),
    ((3, 1), (2, 1), (1, 1), (0, 1), (0, 0), (1, 0), (2, 0), (3, 0)),
)


def spots(path):
    return [(2 * x + core, dep) for x, dep in path for core in ((0, 1) if dep else (1, 0))]


PLACES = [spots(path) for path in PATHS]


def device_of(slab):
    block, rank = divmod(slab % 256, 16)
    lat, dep = PLACES[block // 8][rank if block % 2 == 0 else 15 - rank]
    return (block * 8 + lat) * 2 + dep


def params():
    return pltpu.CompilerParams(vmem_limit_bytes=VMEM_LIMIT)


def vmem(count):
    return [pl.BlockSpec(memory_space=pltpu.VMEM)] * count


def smem(count):
    return [pl.BlockSpec(memory_space=pltpu.SMEM)] * count


def is_odd(me):
    block, lat, dep = lax.div(me, 16), lax.rem(lax.div(me, 2), 8), lax.rem(me, 2)
    return lax.rem(block + lat + dep + 1, 2)


def block_rank(block, chunk):
    low, high = (places.index((chunk // 2, chunk % 2)) for places in PLACES)
    rank = low if low == high else jnp.where(block < 8, low, high)
    odd = lax.rem(block, 2)
    return rank + odd * (15 - 2 * rank)


def pack_kernel(me_ref, rows_ref, out_ref, turned):
    block = lax.div(me_ref[0], 16)
    for q in range(3):
        for half in range(2):
            tile = rows_ref[128 * q : 128 * q + 128, half * 128 : half * 128 + 128]
            turned[q, half * 128 : half * 128 + 128, :] = tile.T
    for chunk in range(16):
        at = pl.multiple_of(block_rank(block, chunk) * 16, 16)
        for q in range(3):
            out_ref[chunk, q * 16 : q * 16 + 16, :] = turned[q, pl.ds(at, 16), :]


def lanes():
    return lax.broadcasted_iota(jnp.int32, (8, 128), 1)


def pick(value, index):
    return jnp.take_along_axis(value, index, axis=1, mode="promise_in_bounds")


def share(own_ref, to_chip, to_next):
    for i in range(HALO):
        to_chip[i] = own_ref[OWN - 1 - i]
        to_next[i] = own_ref[i]


def local(odd, o):
    return o + odd * (OWN - 1 - 2 * o)


def unpack_kernel(me_ref, in_ref, own_ref, to_chip, to_next):
    lane = lanes()
    row, depth = lane // 16, lane % 16
    place = (depth % 8) * 8 + row
    upper = depth >= 8
    odd = is_odd(me_ref[0])
    for o in range(OWN):
        for q in range(3):
            parts = [in_ref[pl.ds(d * 48 + q * 16 + o, 8, stride=96), :] for d in range(2)]
            for half in range(2):
                index = place + 64 * half
                own_ref[local(odd, o), 2 * q + half] = jnp.where(upper, pick(parts[1], index), pick(parts[0], index))
    share(own_ref, to_chip, to_next)


def plane_masks(step):
    lane = lanes()
    row = lax.broadcasted_iota(jnp.int32, (8, 128), 0)
    depth = lane % 16
    return (
        lane < 16 * step,
        row == 7,
        lane >= 128 - 16 * step,
        row == 0,
        jnp.where(depth >= 16 - step, 0.0, 1.0).astype(F32),
        jnp.where(depth < step, 0.0, 1.0).astype(F32),
    )


def plane_near(v, masks, step):
    first, top, last, bottom, keep_up, keep_down = masks
    zero = jnp.zeros_like(v)
    above = jnp.where(first, jnp.where(top, zero, pltpu.roll(v, 7, 0)), v)
    below = jnp.where(last, jnp.where(bottom, zero, pltpu.roll(v, 1, 0)), v)
    total = pltpu.roll(above, 128 - 16 * step, 1) + pltpu.roll(below, 16 * step, 1)
    return total + (pltpu.roll(v, 128 - step, 1) * keep_up + pltpu.roll(v, step, 1) * keep_down)


def stencil(start, stop, u_ref, sea, coupling, masks, step, emit):
    def load(w):
        u = [u_ref[w, f] for f in range(FIELDS)]
        s = sea(w)
        return u, [s * x for x in u]

    _, before = load(start - 1)
    u, v = load(start)
    for w in range(start, stop):
        u_next, after = load(w + 1)
        for f in range(FIELDS):
            near = (before[f] + after[f]) + plane_near(v[f], masks, step)
            others = [coupling[f][g] * u[g] for g in range(FIELDS) if g != f]
            emit(w, f, u[f], near, others[0] + others[1] + others[2])
        before, u, v = v, u_next, after


def halves(t):
    lane = lanes()
    t = t + jnp.where(lane % 2 == 0, pltpu.roll(t, 127, 1), pltpu.roll(t, 1, 1))
    return t + jnp.where((lane // 16) % 2 == 0, pltpu.roll(t, 112, 1), pltpu.roll(t, 16, 1))


def fine_passes(coupling, coeffs, u_a, u_b):
    gain, size, b_sum = coeffs
    masks = plane_masks(1)

    def sea(w):
        return gain[w, FIELDS]

    def sweep_into(target):
        def emit(w, f, u, near, off):
            target[w, f] = (0.2 * u + b_sum[w, f]) + gain[w, f] * (near - off)

        return emit

    def residual(w, f, u, near, off):
        u_b[w, f] = ((b_sum[w, f] - OMEGA * u) + gain[w, f] * (near - off)) * size[w, f]

    def a_to_b(start, stop):
        stencil(start, stop, u_a, sea, coupling, masks, 1, sweep_into(u_b))

    def b_to_a(start, stop):
        stencil(start, stop, u_b, sea, coupling, masks, 1, sweep_into(u_a))

    def rest(start, stop):
        stencil(start, stop, u_a, sea, coupling, masks, 1, residual)

    return a_to_b, b_to_a, rest


def inner_passes(coupling, coeffs, u_a, u_b):
    for turn, one in enumerate(fine_passes(coupling, coeffs, u_a, u_b)):
        one(BASE + 1 + turn, BASE + OWN - 1 - turn)


def chip_passes(coupling, coeffs, u_a, u_b):
    for turn, one in enumerate(fine_passes(coupling, coeffs, u_a, u_b)):
        one(BASE + OWN - 1 - turn, BASE + OWN + HALO - 1 - turn)


def solve(coupling, coeffs, gain_c, u_a, u_b, e_a, e_b, rhs_c):
    gain = coeffs[0]
    passes = fine_passes(coupling, coeffs, u_a, u_b)
    for turn, one in enumerate(passes):
        one(BASE - HALO + 1 + turn, BASE + 1 + turn)

    masks_c = plane_masks(2)

    def sea_c(c):
        return gain_c[c, FIELDS]

    def coarse_into(target):
        def emit(c, f, e, near, off):
            target[c, f] = (0.2 * e + rhs_c[c, f]) + gain_c[c, f] * (0.25 * near - off)

        return emit

    def restrict(c, carry):
        s = sea_c(c)
        for f in range(FIELDS):
            mean = halves(u_b[2 * c, f] + u_b[2 * c + 1, f]) * 0.125
            first = (gain_c[c, f] + (1.0 - s) * OMEGA) * (s * mean)
            rhs_c[c, f] = first
            e_a[c, f] = first
        return carry

    lax.fori_loop(2, 20, restrict, 0, unroll=UNROLL[0])
    stencil(3, 19, e_a, sea_c, coupling, masks_c, 2, coarse_into(e_b))
    stencil(4, 18, e_b, sea_c, coupling, masks_c, 2, coarse_into(e_a))
    stencil(5, 17, e_a, sea_c, coupling, masks_c, 2, coarse_into(e_b))

    def correct(c, carry):
        for f in range(FIELDS):
            e = e_b[c, f]
            for w in (2 * c, 2 * c + 1):
                u_a[w, f] = u_a[w, f] + gain[w, FIELDS] * e
        return carry

    lax.fori_loop(5, 17, correct, 0, unroll=UNROLL[1])
    passes[0](12, 32)
    passes[1](13, 31)
    passes[0](14, 30)


def each_plane(ref, count, place, visit):
    def body(i, carry):
        visit(place(i), ref, i)
        return carry

    lax.fori_loop(0, count, body, 0, unroll=UNROLL[2])


def own_place(i):
    return BASE + i


def chip_place(i):
    return BASE + OWN + i


def next_place(i):
    return BASE - 1 - i


def read_coupling(coupling_ref):
    return [[coupling_ref[f, g] for g in range(FIELDS)] for f in range(FIELDS)]


def fine_coefficients(table, coupling, coeffs, u_a, kappas):
    gain, size, b_sum = coeffs

    def visit(w, ref, at):
        s = ref[at, 4]
        kind = ref[at, 5]
        gain[w, FIELDS] = s
        hits = [kind == float(c) for c in range(CLASSES)]
        for f in range(FIELDS):
            kappa = jnp.zeros_like(s)
            for c in range(CLASSES):
                kappa = jnp.where(hits[c], table[c][f], kappa)
            diag = s * (kappa + (coupling[f][f] + 6.0)) + (1.0 - s)
            rate = OMEGA / diag
            first = rate * (s * ref[at, f])
            gain[w, f] = s * rate
            size[w, f] = diag * (1.0 / OMEGA)
            b_sum[w, f] = first
            u_a[w, f] = first
            kappas[w, f] = kappa

    return visit


def coarse_coefficients(coupling, gain, gain_c, kappas):
    def visit(c, carry):
        s = jnp.minimum(halves(gain[2 * c, FIELDS] + gain[2 * c + 1, FIELDS]), 1.0)
        gain_c[c, FIELDS] = s
        for f in range(FIELDS):
            kappa = halves(kappas[2 * c, f] + kappas[2 * c + 1, f]) * 0.125
            diag = s * (kappa + (coupling[f][f] + 1.5)) + (1.0 - s)
            gain_c[c, f] = s * (OMEGA / diag)
        return carry

    return visit


def read_table(table_ref):
    return [[table_ref[c, f] for f in range(FIELDS)] for c in range(CLASSES)]


def first_part(table_ref, coupling_ref, ref, place, cells, coeffs, gain_c, u_a, kappas):
    coupling = read_coupling(coupling_ref)
    each_plane(ref, ref.shape[0], place, fine_coefficients(read_table(table_ref), coupling, coeffs, u_a, kappas))
    visit = coarse_coefficients(coupling, coeffs[0], gain_c, kappas)
    start, stop = cells
    lax.fori_loop(start, stop, visit, 0, unroll=UNROLL[3])
    return coupling


def inner_first_kernel(table_ref, coupling_ref, own_ref, gain, size, b_sum, gain_c, u_a, u_b):
    coeffs = (gain, size, b_sum)
    coupling = first_part(table_ref, coupling_ref, own_ref, own_place, (7, 15), coeffs, gain_c, u_a, u_b)
    inner_passes(coupling, coeffs, u_a, u_b)


def chip_first_kernel(table_ref, coupling_ref, chip_ref, *refs):
    gain, size, b_sum, gain_c, u_a, u_b, kappas = refs[6:]
    coeffs = (gain, size, b_sum)
    coupling = first_part(table_ref, coupling_ref, chip_ref, chip_place, (15, 20), coeffs, gain_c, u_a, kappas)
    chip_passes(coupling, coeffs, u_a, u_b)


def first_kernel(table_ref, coupling_ref, next_ref, *refs):
    gain, size, b_sum, gain_c, u_a, u_b, out_ref, to_chip, to_next, e_a, e_b, rhs_c, kappas = refs[6:]
    coeffs = (gain, size, b_sum)
    coupling = first_part(table_ref, coupling_ref, next_ref, next_place, (2, 7), coeffs, gain_c, u_a, kappas)
    solve(coupling, coeffs, gain_c, u_a, u_b, e_a, e_b, rhs_c)
    out_ref[...] = u_b[BASE : BASE + OWN]
    share(out_ref, to_chip, to_next)


def second_start(coeffs, u_a):
    gain, _, b_sum = coeffs

    def visit(w, ref, at):
        land = (1.0 - gain[w, FIELDS]) * OMEGA
        for f in range(FIELDS):
            first = (gain[w, f] + land) * ref[at, f]
            b_sum[w, f] = first
            u_a[w, f] = first

    return visit


def send_rows(odd, kind, plane_of, out_ref):
    lane = lanes()
    place = (lane % 8) * 16 + (lane // 8) % 8
    lower = lane < 64
    for o in range(OWN):
        for q in range(2):
            pair = [plane_of(local(odd, o), 2 * q + h) for h in range(2)]
            for d in range(2):
                index = place + 8 * d
                rows = jnp.where(lower, pick(pair[0], index), pick(pair[1], index))
                out_ref[pl.ds(d * 64 + kind * 32 + q * 16 + o, 8, stride=128), :] = rows


def inner_second_kernel(me_ref, coupling_ref, own_ref, gain, size, b_sum, u_a, u_b, out_ref):
    coeffs = (gain, size, b_sum)
    each_plane(own_ref, OWN, own_place, second_start(coeffs, u_a))
    inner_passes(read_coupling(coupling_ref), coeffs, u_a, u_b)
    send_rows(is_odd(me_ref[0]), 0, lambda at, f: own_ref[at, f], out_ref)


def chip_second_kernel(coupling_ref, chip_ref, gain, size, *refs):
    b_sum, u_a, u_b = refs[3:]
    coeffs = (gain, size, b_sum)
    each_plane(chip_ref, HALO, chip_place, second_start(coeffs, u_a))
    chip_passes(read_coupling(coupling_ref), coeffs, u_a, u_b)


def second_kernel(me_ref, coupling_ref, next_ref, gain, size, gain_c, *refs):
    b_sum, u_a, u_b, out_ref, e_a, e_b, rhs_c = refs[4:]
    coeffs = (gain, size, b_sum)
    each_plane(next_ref, HALO, next_place, second_start(coeffs, u_a))
    solve(read_coupling(coupling_ref), coeffs, gain_c, u_a, u_b, e_a, e_b, rhs_c)
    send_rows(is_odd(me_ref[0]), 1, lambda at, f: u_b[BASE + at, f], out_ref)


def finish_kernel(me_ref, in_ref, first_ref, second_ref, turned):
    block = lax.div(me_ref[0], 16)
    for k, out_ref in enumerate((first_ref, second_ref)):
        for q in range(2):
            for chunk in range(16):
                at = pl.multiple_of(block_rank(block, chunk) * 16, 16)
                turned[2 * k + q, pl.ds(at, 16), :] = in_ref[chunk, k * 32 + q * 16 : k * 32 + q * 16 + 16, :]
            for half in range(2):
                pair = turned[2 * k + q, half * 128 : half * 128 + 128, :].T
                for h in range(2):
                    out_ref[2 * q + h, :, :, half * 128 : half * 128 + 128] = pair[64 * h : 64 * h + 64].reshape(8, 8, 128)


def planes(count, kinds=FIELDS):
    return jax.ShapeDtypeStruct((count, kinds, 8, 128), F32)


def scratch(count, kinds=FIELDS):
    return pltpu.VMEM((count, kinds, 8, 128), F32)


def per_device(source, sea_mask, classes, kappa_table, coupling):
    me = lax.axis_index(AXES).astype(jnp.int32).reshape(1)
    chips = [(device_of(g ^ 1), device_of(g)) for g in range(256)]
    nexts = [(device_of(((g + 1) ^ 1) - 1), device_of(g)) for g in range(256)]

    def trade(to_chip, to_next):
        from_next = lax.ppermute(to_next, AXES, nexts)
        return lax.ppermute(to_chip, AXES, chips), from_next

    sent = pl.pallas_call(
        pack_kernel,
        out_shape=jax.ShapeDtypeStruct((16, 48, 128), F32),
        in_specs=smem(1) + vmem(1),
        out_specs=vmem(1)[0],
        scratch_shapes=[pltpu.VMEM((3, 256, 128), F32)],
        compiler_params=params(),
        name="pack",
    )(me, jnp.concatenate([x.astype(F32).reshape(-1, 256) for x in (source, sea_mask, classes)]))
    got = lax.all_to_all(sent, ("lat", "dep"), 0, 0, tiled=False)
    def call(kernel, given, numbers, state, more, work, name):
        return pl.pallas_call(
            kernel,
            out_shape=tuple(state) + tuple(more),
            in_specs=smem(numbers) + vmem(len(given) - numbers + len(state)),
            out_specs=tuple(vmem(len(state) + len(more))),
            scratch_shapes=work,
            input_output_aliases={len(given) + i: i for i in range(len(state))},
            compiler_params=params(),
            cost_estimate=pl.CostEstimate(flops=40_000_000, bytes_accessed=8_000_000, transcendentals=0),
            name=name,
        )(*given, *state)

    halo = [planes(HALO), planes(HALO)]
    coarse = [scratch(COARSE_WIDE)] * 3
    rows = jax.ShapeDtypeStruct((1024, 128), F32)
    given = [me, got.reshape(768, 128)]
    own, to_chip, to_next = call(unpack_kernel, given, 1, [], [planes(OWN, 6), planes(HALO, 6), planes(HALO, 6)], [], "unpack")
    mate, beyond = trade(to_chip, to_next)

    fresh = [planes(WIDE, 5), planes(WIDE), planes(WIDE), planes(COARSE_WIDE, 5), planes(WIDE), planes(WIDE)]
    numbers = [kappa_table, coupling]
    state = call(inner_first_kernel, numbers + [own], 2, [], fresh, [], "inner_first")
    state = call(chip_first_kernel, numbers + [mate], 2, state, [], [scratch(WIDE)], "chip_first")
    more = [planes(OWN)] + halo
    state = call(first_kernel, numbers + [beyond], 2, state, more, coarse + [scratch(WIDE)], "first")
    gain, size, _, gain_c, _, _, first, to_chip, to_next = state
    mate, beyond = trade(to_chip, to_next)

    fresh = [planes(WIDE), planes(WIDE), planes(WIDE), rows]
    state = call(inner_second_kernel, [me, coupling, first, gain, size], 2, [], fresh, [], "inner_second")
    sent = state[3]
    state = call(chip_second_kernel, [coupling, mate, gain, size], 1, state[:3], [], [], "chip_second")
    state = call(second_kernel, [me, coupling, beyond, gain, size, gain_c], 2, list(state) + [sent], [], coarse, "second")
    sent = state[3]
    got = lax.all_to_all(sent.reshape(16, 64, 128), ("lat", "dep"), 0, 0, tiled=False)
    out = jax.ShapeDtypeStruct((FIELDS, 8, 8, 256), F32)
    return pl.pallas_call(
        finish_kernel,
        out_shape=(out, out),
        in_specs=smem(1) + vmem(1),
        out_specs=tuple(vmem(2)),
        scratch_shapes=[pltpu.VMEM((4, 256, 128), F32)],
        compiler_params=params(),
        name="finish",
    )(me, got)


def solution(mesh):
    return jax.shard_map(
        per_device,
        mesh=mesh,
        in_specs=(
            P(None, "dep", "lat", "lon"),
            P("dep", "lat", "lon"),
            P("dep", "lat", "lon"),
            P(),
            P(),
        ),
        out_specs=(P(None, "dep", "lat", "lon"), P(None, "dep", "lat", "lon")),
        check_vma=False,
    )
```

```python
import functools

import jax
import jax.numpy as jnp
from jax import lax
from jax.experimental import pallas as pl
from jax.experimental.pallas import tpu as pltpu
from jax.sharding import PartitionSpec as P


FIELDS = 4
CLASSES = 8
OMEGA = 0.8
OWN = 16
HALO = 13
BASE = 14
WIDE = OWN + 2 * BASE
COARSE_WIDE = WIDE // 2
UNROLL = (9, 12, 13, 4)
AXES = ("lon", "lat", "dep")
F32 = jnp.float32
VMEM_LIMIT = 48 * 1024 * 1024


PATHS = (
    ((3, 1), (2, 1), (1, 1), (0, 1), (0, 0), (1, 0), (2, 0), (3, 0)),
    ((3, 1), (2, 1), (1, 1), (0, 1), (0, 0), (1, 0), (2, 0), (3, 0)),
)


def spots(path):
    return [(2 * x + core, dep) for x, dep in path for core in ((0, 1) if dep else (1, 0))]


PLACES = [spots(path) for path in PATHS]


def device_of(slab):
    block, rank = divmod(slab % 256, 16)
    lat, dep = PLACES[block // 8][rank if block % 2 == 0 else 15 - rank]
    return (block * 8 + lat) * 2 + dep


def params():
    return pltpu.CompilerParams(vmem_limit_bytes=VMEM_LIMIT)


def vmem(count):
    return [pl.BlockSpec(memory_space=pltpu.VMEM)] * count


def smem(count):
    return [pl.BlockSpec(memory_space=pltpu.SMEM)] * count


def is_odd(me):
    block, lat, dep = lax.div(me, 16), lax.rem(lax.div(me, 2), 8), lax.rem(me, 2)
    return lax.rem(block + lat + dep + 1, 2)


def block_rank(block, chunk):
    low, high = (places.index((chunk // 2, chunk % 2)) for places in PLACES)
    rank = low if low == high else jnp.where(block < 8, low, high)
    odd = lax.rem(block, 2)
    return rank + odd * (15 - 2 * rank)


def pack_kernel(me_ref, rows_ref, out_ref, turned):
    block = lax.div(me_ref[0], 16)
    for q in range(3):
        for half in range(2):
            tile = rows_ref[128 * q : 128 * q + 128, half * 128 : half * 128 + 128]
            turned[q, half * 128 : half * 128 + 128, :] = tile.T
    for chunk in range(16):
        at = pl.multiple_of(block_rank(block, chunk) * 16, 16)
        for q in range(3):
            out_ref[chunk, q * 16 : q * 16 + 16, :] = turned[q, pl.ds(at, 16), :]


def lanes():
    return lax.broadcasted_iota(jnp.int32, (8, 128), 1)


def pick(value, index):
    return jnp.take_along_axis(value, index, axis=1, mode="promise_in_bounds")


def share(own_ref, to_chip, to_next):
    for i in range(HALO):
        to_chip[i] = own_ref[OWN - 1 - i]
        to_next[i] = own_ref[i]


def local(odd, o):
    return o + odd * (OWN - 1 - 2 * o)


def unpack_kernel(me_ref, in_ref, own_ref, to_chip, to_next):
    lane = lanes()
    row, depth = lane // 16, lane % 16
    place = (depth % 8) * 8 + row
    upper = depth >= 8
    odd = is_odd(me_ref[0])
    for o in range(OWN):
        for q in range(3):
            parts = [in_ref[pl.ds(d * 48 + q * 16 + o, 8, stride=96), :] for d in range(2)]
            for half in range(2):
                index = place + 64 * half
                own_ref[local(odd, o), 2 * q + half] = jnp.where(upper, pick(parts[1], index), pick(parts[0], index))
    share(own_ref, to_chip, to_next)


def plane_masks(step):
    lane = lanes()
    row = lax.broadcasted_iota(jnp.int32, (8, 128), 0)
    depth = lane % 16
    return (
        lane < 16 * step,
        row == 7,
        lane >= 128 - 16 * step,
        row == 0,
        jnp.where(depth >= 16 - step, 0.0, 1.0).astype(F32),
        jnp.where(depth < step, 0.0, 1.0).astype(F32),
    )


def plane_near(v, masks, step):
    first, top, last, bottom, keep_up, keep_down = masks
    zero = jnp.zeros_like(v)
    above = jnp.where(first, jnp.where(top, zero, pltpu.roll(v, 7, 0)), v)
    below = jnp.where(last, jnp.where(bottom, zero, pltpu.roll(v, 1, 0)), v)
    total = pltpu.roll(above, 128 - 16 * step, 1) + pltpu.roll(below, 16 * step, 1)
    return total + (pltpu.roll(v, 128 - step, 1) * keep_up + pltpu.roll(v, step, 1) * keep_down)


def stencil(start, stop, u_ref, sea, coupling, masks, step, emit):
    def load(w):
        u = [u_ref[w, f] for f in range(FIELDS)]
        s = sea(w)
        return u, [s * x for x in u]

    _, before = load(start - 1)
    u, v = load(start)
    for w in range(start, stop):
        u_next, after = load(w + 1)
        for f in range(FIELDS):
            near = (before[f] + after[f]) + plane_near(v[f], masks, step)
            others = [coupling[f][g] * u[g] for g in range(FIELDS) if g != f]
            emit(w, f, u[f], near, others[0] + others[1] + others[2])
        before, u, v = v, u_next, after


class Places:
    def __init__(self):
        lane = lanes()
        self.swaps = [jnp.bitwise_xor(lane, x) for x in (1, 16, 17)]
        self.even_depth = lane % 2 == 0
        self.even_lat = (lane // 16) % 2 == 0

    def turn(self, value, x):
        return pick(value, self.swaps[x - 1]) if x else value

    def choose(self, values):
        low = jnp.where(self.even_depth, values[0], values[1])
        return jnp.where(self.even_lat, low, jnp.where(self.even_depth, values[2], values[3]))

    def gather(self, t):
        pairs = []
        for x, y in ((t[0], t[1]), (t[2], t[3])):
            pairs.append(jnp.where(self.even_depth, x, y) + self.turn(jnp.where(self.even_depth, y, x), 1))
        x, y = pairs
        return jnp.where(self.even_lat, x, y) + self.turn(jnp.where(self.even_lat, y, x), 2)

    def total(self, t):
        t = t + self.turn(t, 1)
        return t + self.turn(t, 2)

    def spread(self, packed):
        turned = [self.turn(packed, x) for x in range(4)]
        return [self.choose([turned[p ^ f] for p in range(4)]) for f in range(FIELDS)]


def coarse_stencil(start, stop, e_ref, target, gain_c, rhs_c, coupling, places):
    masks = plane_masks(2)
    mix = [places.choose([jnp.full((8, 128), coupling[f][f ^ x], F32) for f in range(FIELDS)]) for x in range(1, 4)]

    def load(c):
        e = e_ref[c, 0]
        return e, gain_c[c, 1] * e

    _, before = load(start - 1)
    e, v = load(start)
    for c in range(start, stop):
        e_next, after = load(c + 1)
        near = (before + after) + plane_near(v, masks, 2)
        off = mix[0] * places.turn(e, 1) + mix[1] * places.turn(e, 2) + mix[2] * places.turn(e, 3)
        target[c, 0] = (0.2 * e + rhs_c[c, 0]) + gain_c[c, 0] * (0.25 * near - off)
        before, e, v = v, e_next, after


def fine_passes(coupling, coeffs, u_a, u_b):
    gain, size, b_sum = coeffs
    masks = plane_masks(1)

    def sea(w):
        return gain[w, FIELDS]

    def sweep_into(target):
        def emit(w, f, u, near, off):
            target[w, f] = (0.2 * u + b_sum[w, f]) + gain[w, f] * (near - off)

        return emit

    def residual(w, f, u, near, off):
        u_b[w, f] = ((b_sum[w, f] - OMEGA * u) + gain[w, f] * (near - off)) * size[w, f]

    def a_to_b(start, stop):
        stencil(start, stop, u_a, sea, coupling, masks, 1, sweep_into(u_b))

    def b_to_a(start, stop):
        stencil(start, stop, u_b, sea, coupling, masks, 1, sweep_into(u_a))

    def rest(start, stop):
        stencil(start, stop, u_a, sea, coupling, masks, 1, residual)

    return a_to_b, b_to_a, rest


def inner_passes(coupling, coeffs, u_a, u_b):
    for turn, one in enumerate(fine_passes(coupling, coeffs, u_a, u_b)):
        one(BASE + 1 + turn, BASE + OWN - 1 - turn)


def chip_passes(coupling, coeffs, u_a, u_b):
    for turn, one in enumerate(fine_passes(coupling, coeffs, u_a, u_b)):
        one(BASE + OWN - 1 - turn, BASE + OWN + HALO - 1 - turn)


def solve(coupling, coeffs, gain_c, u_a, u_b, e_a, e_b, rhs_c):
    gain = coeffs[0]
    passes = fine_passes(coupling, coeffs, u_a, u_b)
    for turn, one in enumerate(passes):
        one(BASE - HALO + 1 + turn, BASE + 1 + turn)

    places = Places()

    def restrict(c, carry):
        s = gain_c[c, 1]
        mean = places.gather([u_b[2 * c, f] + u_b[2 * c + 1, f] for f in range(FIELDS)]) * 0.125
        first = (gain_c[c, 0] + (1.0 - s) * OMEGA) * (s * mean)
        rhs_c[c, 0] = first
        e_a[c, 0] = first
        return carry

    lax.fori_loop(2, 20, restrict, 0, unroll=UNROLL[0])
    coarse_stencil(3, 19, e_a, e_b, gain_c, rhs_c, coupling, places)
    coarse_stencil(4, 18, e_b, e_a, gain_c, rhs_c, coupling, places)
    coarse_stencil(5, 17, e_a, e_b, gain_c, rhs_c, coupling, places)

    def correct(c, carry):
        e = places.spread(e_b[c, 0])
        for w in (2 * c, 2 * c + 1):
            for f in range(FIELDS):
                u_a[w, f] = u_a[w, f] + gain[w, FIELDS] * e[f]
        return carry

    lax.fori_loop(5, 17, correct, 0, unroll=UNROLL[1])
    passes[0](12, 32)
    passes[1](13, 31)
    passes[0](14, 30)


def each_plane(ref, count, place, visit):
    def body(i, carry):
        visit(place(i), ref, i)
        return carry

    lax.fori_loop(0, count, body, 0, unroll=UNROLL[2])


def own_place(i):
    return BASE + i


def chip_place(i):
    return BASE + OWN + i


def next_place(i):
    return BASE - 1 - i


def read_coupling(coupling_ref):
    return [[coupling_ref[f, g] for g in range(FIELDS)] for f in range(FIELDS)]


def fine_coefficients(table, coupling, coeffs, u_a, kappas):
    gain, size, b_sum = coeffs

    def visit(w, ref, at):
        s = ref[at, 4]
        kind = ref[at, 5]
        gain[w, FIELDS] = s
        hits = [kind == float(c) for c in range(CLASSES)]
        for f in range(FIELDS):
            kappa = jnp.zeros_like(s)
            for c in range(CLASSES):
                kappa = jnp.where(hits[c], table[c][f], kappa)
            diag = s * (kappa + (coupling[f][f] + 6.0)) + (1.0 - s)
            rate = OMEGA / diag
            first = rate * (s * ref[at, f])
            gain[w, f] = s * rate
            size[w, f] = diag * (1.0 / OMEGA)
            b_sum[w, f] = first
            u_a[w, f] = first
            kappas[w, f] = kappa

    return visit


def coarse_coefficients(coupling, gain, gain_c, kappas):
    places = Places()
    own = places.choose([jnp.full((8, 128), coupling[f][f] + 1.5, F32) for f in range(FIELDS)])

    def visit(c, carry):
        s = jnp.minimum(places.total(gain[2 * c, FIELDS] + gain[2 * c + 1, FIELDS]), 1.0)
        kappa = places.gather([kappas[2 * c, f] + kappas[2 * c + 1, f] for f in range(FIELDS)]) * 0.125
        diag = s * (kappa + own) + (1.0 - s)
        gain_c[c, 0] = s * (OMEGA / diag)
        gain_c[c, 1] = s
        return carry

    return visit


def read_table(table_ref):
    return [[table_ref[c, f] for f in range(FIELDS)] for c in range(CLASSES)]


def first_part(table_ref, coupling_ref, ref, place, cells, coeffs, gain_c, u_a, kappas):
    coupling = read_coupling(coupling_ref)
    each_plane(ref, ref.shape[0], place, fine_coefficients(read_table(table_ref), coupling, coeffs, u_a, kappas))
    visit = coarse_coefficients(coupling, coeffs[0], gain_c, kappas)
    start, stop = cells
    lax.fori_loop(start, stop, visit, 0, unroll=UNROLL[3])
    return coupling


def inner_first_kernel(table_ref, coupling_ref, own_ref, gain, size, b_sum, gain_c, u_a, u_b):
    coeffs = (gain, size, b_sum)
    coupling = first_part(table_ref, coupling_ref, own_ref, own_place, (7, 15), coeffs, gain_c, u_a, u_b)
    inner_passes(coupling, coeffs, u_a, u_b)


def chip_first_kernel(table_ref, coupling_ref, chip_ref, *refs):
    gain, size, b_sum, gain_c, u_a, u_b, kappas = refs[6:]
    coeffs = (gain, size, b_sum)
    coupling = first_part(table_ref, coupling_ref, chip_ref, chip_place, (15, 20), coeffs, gain_c, u_a, kappas)
    chip_passes(coupling, coeffs, u_a, u_b)


def first_kernel(table_ref, coupling_ref, next_ref, *refs):
    gain, size, b_sum, gain_c, u_a, u_b, out_ref, to_chip, to_next, e_a, e_b, rhs_c, kappas = refs[6:]
    coeffs = (gain, size, b_sum)
    coupling = first_part(table_ref, coupling_ref, next_ref, next_place, (2, 7), coeffs, gain_c, u_a, kappas)
    solve(coupling, coeffs, gain_c, u_a, u_b, e_a, e_b, rhs_c)
    out_ref[...] = u_b[BASE : BASE + OWN]
    share(out_ref, to_chip, to_next)


def second_start(coeffs, u_a):
    gain, _, b_sum = coeffs

    def visit(w, ref, at):
        land = (1.0 - gain[w, FIELDS]) * OMEGA
        for f in range(FIELDS):
            first = (gain[w, f] + land) * ref[at, f]
            b_sum[w, f] = first
            u_a[w, f] = first

    return visit


def send_rows(odd, kind, plane_of, out_ref):
    lane = lanes()
    place = (lane % 8) * 16 + (lane // 8) % 8
    lower = lane < 64
    for o in range(OWN):
        for q in range(2):
            pair = [plane_of(local(odd, o), 2 * q + h) for h in range(2)]
            for d in range(2):
                index = place + 8 * d
                rows = jnp.where(lower, pick(pair[0], index), pick(pair[1], index))
                out_ref[pl.ds(d * 64 + kind * 32 + q * 16 + o, 8, stride=128), :] = rows


def inner_second_kernel(me_ref, coupling_ref, own_ref, gain, size, b_sum, u_a, u_b, out_ref):
    coeffs = (gain, size, b_sum)
    each_plane(own_ref, OWN, own_place, second_start(coeffs, u_a))
    inner_passes(read_coupling(coupling_ref), coeffs, u_a, u_b)
    send_rows(is_odd(me_ref[0]), 0, lambda at, f: own_ref[at, f], out_ref)


def chip_second_kernel(coupling_ref, chip_ref, gain, size, *refs):
    b_sum, u_a, u_b = refs[3:]
    coeffs = (gain, size, b_sum)
    each_plane(chip_ref, HALO, chip_place, second_start(coeffs, u_a))
    chip_passes(read_coupling(coupling_ref), coeffs, u_a, u_b)


def second_kernel(me_ref, coupling_ref, next_ref, gain, size, gain_c, *refs):
    b_sum, u_a, u_b, out_ref, e_a, e_b, rhs_c = refs[4:]
    coeffs = (gain, size, b_sum)
    each_plane(next_ref, HALO, next_place, second_start(coeffs, u_a))
    solve(read_coupling(coupling_ref), coeffs, gain_c, u_a, u_b, e_a, e_b, rhs_c)
    send_rows(is_odd(me_ref[0]), 1, lambda at, f: u_b[BASE + at, f], out_ref)


def finish_kernel(me_ref, in_ref, first_ref, second_ref, turned):
    block = lax.div(me_ref[0], 16)
    for k, out_ref in enumerate((first_ref, second_ref)):
        for q in range(2):
            for chunk in range(16):
                at = pl.multiple_of(block_rank(block, chunk) * 16, 16)
                turned[2 * k + q, pl.ds(at, 16), :] = in_ref[chunk, k * 32 + q * 16 : k * 32 + q * 16 + 16, :]
            for half in range(2):
                pair = turned[2 * k + q, half * 128 : half * 128 + 128, :].T
                for h in range(2):
                    out_ref[2 * q + h, :, :, half * 128 : half * 128 + 128] = pair[64 * h : 64 * h + 64].reshape(8, 8, 128)


def planes(count, kinds=FIELDS):
    return jax.ShapeDtypeStruct((count, kinds, 8, 128), F32)


def scratch(count, kinds=FIELDS):
    return pltpu.VMEM((count, kinds, 8, 128), F32)


def per_device(source, sea_mask, classes, kappa_table, coupling):
    me = lax.axis_index(AXES).astype(jnp.int32).reshape(1)
    chips = [(device_of(g ^ 1), device_of(g)) for g in range(256)]
    nexts = [(device_of(((g + 1) ^ 1) - 1), device_of(g)) for g in range(256)]

    def trade(to_chip, to_next):
        from_next = lax.ppermute(to_next, AXES, nexts)
        return lax.ppermute(to_chip, AXES, chips), from_next

    sent = pl.pallas_call(
        pack_kernel,
        out_shape=jax.ShapeDtypeStruct((16, 48, 128), F32),
        in_specs=smem(1) + vmem(1),
        out_specs=vmem(1)[0],
        scratch_shapes=[pltpu.VMEM((3, 256, 128), F32)],
        compiler_params=params(),
        name="pack",
    )(me, jnp.concatenate([x.astype(F32).reshape(-1, 256) for x in (source, sea_mask, classes)]))
    got = lax.all_to_all(sent, ("lat", "dep"), 0, 0, tiled=False)
    def call(kernel, given, numbers, state, more, work, name):
        return pl.pallas_call(
            kernel,
            out_shape=tuple(state) + tuple(more),
            in_specs=smem(numbers) + vmem(len(given) - numbers + len(state)),
            out_specs=tuple(vmem(len(state) + len(more))),
            scratch_shapes=work,
            input_output_aliases={len(given) + i: i for i in range(len(state))},
            compiler_params=params(),
            cost_estimate=pl.CostEstimate(flops=40_000_000, bytes_accessed=8_000_000, transcendentals=0),
            name=name,
        )(*given, *state)

    halo = [planes(HALO), planes(HALO)]
    coarse = [scratch(COARSE_WIDE, 1)] * 3
    rows = jax.ShapeDtypeStruct((1024, 128), F32)
    given = [me, got.reshape(768, 128)]
    own, to_chip, to_next = call(unpack_kernel, given, 1, [], [planes(OWN, 6), planes(HALO, 6), planes(HALO, 6)], [], "unpack")
    mate, beyond = trade(to_chip, to_next)

    fresh = [planes(WIDE, 5), planes(WIDE), planes(WIDE), planes(COARSE_WIDE, 2), planes(WIDE), planes(WIDE)]
    numbers = [kappa_table, coupling]
    state = call(inner_first_kernel, numbers + [own], 2, [], fresh, [], "inner_first")
    state = call(chip_first_kernel, numbers + [mate], 2, state, [], [scratch(WIDE)], "chip_first")
    more = [planes(OWN)] + halo
    state = call(first_kernel, numbers + [beyond], 2, state, more, coarse + [scratch(WIDE)], "first")
    gain, size, _, gain_c, _, _, first, to_chip, to_next = state
    mate, beyond = trade(to_chip, to_next)

    fresh = [planes(WIDE), planes(WIDE), planes(WIDE), rows]
    state = call(inner_second_kernel, [me, coupling, first, gain, size], 2, [], fresh, [], "inner_second")
    sent = state[3]
    state = call(chip_second_kernel, [coupling, mate, gain, size], 1, state[:3], [], [], "chip_second")
    state = call(second_kernel, [me, coupling, beyond, gain, size, gain_c], 2, list(state) + [sent], [], coarse, "second")
    sent = state[3]
    got = lax.all_to_all(sent.reshape(16, 64, 128), ("lat", "dep"), 0, 0, tiled=False)
    out = jax.ShapeDtypeStruct((FIELDS, 8, 8, 256), F32)
    return pl.pallas_call(
        finish_kernel,
        out_shape=(out, out),
        in_specs=smem(1) + vmem(1),
        out_specs=tuple(vmem(2)),
        scratch_shapes=[pltpu.VMEM((4, 256, 128), F32)],
        compiler_params=params(),
        name="finish",
    )(me, got)


def solution(mesh):
    return jax.shard_map(
        per_device,
        mesh=mesh,
        in_specs=(
            P(None, "dep", "lat", "lon"),
            P("dep", "lat", "lon"),
            P("dep", "lat", "lon"),
            P(),
            P(),
        ),
        out_specs=(P(None, "dep", "lat", "lon"), P(None, "dep", "lat", "lon")),
        check_vma=False,
    )
```

```python
import functools

import jax
import jax.numpy as jnp
from jax import lax
from jax.experimental import pallas as pl
from jax.experimental.pallas import tpu as pltpu
from jax.sharding import PartitionSpec as P


FIELDS = 4
CLASSES = 8
OMEGA = 0.8
OWN = 16
HALO = 13
BASE = 14
WIDE = OWN + 2 * BASE
COARSE_WIDE = WIDE // 2
UNROLL = (9, 12, 13, 4)
AXES = ("lon", "lat", "dep")
F32 = jnp.float32
VMEM_LIMIT = 48 * 1024 * 1024


PATHS = (
    ((1, 0), (2, 0), (3, 0), (0, 0), (0, 1), (3, 1), (2, 1), (1, 1)),
    ((1, 0), (2, 0), (3, 0), (0, 0), (0, 1), (3, 1), (2, 1), (1, 1)),
)


def spots(path):
    return [(2 * x + core, dep) for x, dep in path for core in ((0, 1) if dep else (1, 0))]


PLACES = [spots(path) for path in PATHS]


def device_of(slab):
    block, rank = divmod(slab % 256, 16)
    lat, dep = PLACES[block // 8][rank if block % 2 == 0 else 15 - rank]
    return (block * 8 + lat) * 2 + dep


def params():
    return pltpu.CompilerParams(vmem_limit_bytes=VMEM_LIMIT)


def vmem(count):
    return [pl.BlockSpec(memory_space=pltpu.VMEM)] * count


def smem(count):
    return [pl.BlockSpec(memory_space=pltpu.SMEM)] * count


def is_odd(me):
    block, lat, dep = lax.div(me, 16), lax.rem(lax.div(me, 2), 8), lax.rem(me, 2)
    return lax.rem(block + lat + dep + 1, 2)


def block_rank(block, chunk):
    low, high = (places.index((chunk % 8, chunk // 8)) for places in PLACES)
    rank = low if low == high else jnp.where(block < 8, low, high)
    odd = lax.rem(block, 2)
    return rank + odd * (15 - 2 * rank)


def pack_kernel(me_ref, rows_ref, out_ref, turned):
    block = lax.div(me_ref[0], 16)
    for q in range(3):
        for half in range(2):
            tile = rows_ref[128 * q : 128 * q + 128, half * 128 : half * 128 + 128]
            turned[q, half * 128 : half * 128 + 128, :] = tile.T
    for chunk in range(16):
        at = pl.multiple_of(block_rank(block, chunk) * 16, 16)
        for q in range(3):
            out_ref[chunk, q * 16 : q * 16 + 16, :] = turned[q, pl.ds(at, 16), :]


def lanes():
    return lax.broadcasted_iota(jnp.int32, (8, 128), 1)


def pick(value, index):
    return jnp.take_along_axis(value, index, axis=1, mode="promise_in_bounds")


def share(own_ref, to_chip, to_next):
    for i in range(HALO):
        to_chip[i] = own_ref[OWN - 1 - i]
        to_next[i] = own_ref[i]


def local(odd, o):
    return o + odd * (OWN - 1 - 2 * o)


def unpack_kernel(me_ref, in_ref, own_ref, to_chip, to_next):
    lane = lanes()
    row, depth = lane // 16, lane % 16
    place = (depth % 8) * 8 + row
    upper = depth >= 8
    odd = is_odd(me_ref[0])
    for o in range(OWN):
        for q in range(3):
            parts = [in_ref[pl.ds(d * 384 + q * 16 + o, 8, stride=48), :] for d in range(2)]
            for half in range(2):
                index = place + 64 * half
                own_ref[local(odd, o), 2 * q + half] = jnp.where(upper, pick(parts[1], index), pick(parts[0], index))
    share(own_ref, to_chip, to_next)


def plane_masks(step):
    lane = lanes()
    row = lax.broadcasted_iota(jnp.int32, (8, 128), 0)
    depth = lane % 16
    return (
        lane < 16 * step,
        row == 7,
        lane >= 128 - 16 * step,
        row == 0,
        jnp.where(depth >= 16 - step, 0.0, 1.0).astype(F32),
        jnp.where(depth < step, 0.0, 1.0).astype(F32),
    )


def plane_near(v, masks, step):
    first, top, last, bottom, keep_up, keep_down = masks
    zero = jnp.zeros_like(v)
    above = jnp.where(first, jnp.where(top, zero, pltpu.roll(v, 7, 0)), v)
    below = jnp.where(last, jnp.where(bottom, zero, pltpu.roll(v, 1, 0)), v)
    total = pltpu.roll(above, 128 - 16 * step, 1) + pltpu.roll(below, 16 * step, 1)
    return total + (pltpu.roll(v, 128 - step, 1) * keep_up + pltpu.roll(v, step, 1) * keep_down)


def stencil(start, stop, u_ref, sea, coupling, masks, step, emit):
    def load(w):
        u = [u_ref[w, f] for f in range(FIELDS)]
        s = sea(w)
        return u, [s * x for x in u]

    _, before = load(start - 1)
    u, v = load(start)
    for w in range(start, stop):
        u_next, after = load(w + 1)
        for f in range(FIELDS):
            near = (before[f] + after[f]) + plane_near(v[f], masks, step)
            others = [coupling[f][g] * u[g] for g in range(FIELDS) if g != f]
            emit(w, f, u[f], near, others[0] + others[1] + others[2])
        before, u, v = v, u_next, after


class Places:
    def __init__(self):
        lane = lanes()
        self.swaps = [jnp.bitwise_xor(lane, x) for x in (1, 16, 17)]
        self.even_depth = lane % 2 == 0
        self.even_lat = (lane // 16) % 2 == 0

    def turn(self, value, x):
        return pick(value, self.swaps[x - 1]) if x else value

    def choose(self, values):
        low = jnp.where(self.even_depth, values[0], values[1])
        return jnp.where(self.even_lat, low, jnp.where(self.even_depth, values[2], values[3]))

    def gather(self, t):
        pairs = []
        for x, y in ((t[0], t[1]), (t[2], t[3])):
            pairs.append(jnp.where(self.even_depth, x, y) + self.turn(jnp.where(self.even_depth, y, x), 1))
        x, y = pairs
        return jnp.where(self.even_lat, x, y) + self.turn(jnp.where(self.even_lat, y, x), 2)

    def total(self, t):
        t = t + self.turn(t, 1)
        return t + self.turn(t, 2)

    def spread(self, packed):
        turned = [self.turn(packed, x) for x in range(4)]
        return [self.choose([turned[p ^ f] for p in range(4)]) for f in range(FIELDS)]


def coarse_stencil(start, stop, e_ref, target, gain_c, rhs_c, coupling, places):
    masks = plane_masks(2)
    mix = [places.choose([jnp.full((8, 128), coupling[f][f ^ x], F32) for f in range(FIELDS)]) for x in range(1, 4)]

    def load(c):
        e = e_ref[c, 0]
        return e, gain_c[c, 1] * e

    _, before = load(start - 1)
    e, v = load(start)
    for c in range(start, stop):
        e_next, after = load(c + 1)
        near = (before + after) + plane_near(v, masks, 2)
        off = mix[0] * places.turn(e, 1) + mix[1] * places.turn(e, 2) + mix[2] * places.turn(e, 3)
        target[c, 0] = (0.2 * e + rhs_c[c, 0]) + gain_c[c, 0] * (0.25 * near - off)
        before, e, v = v, e_next, after


def fine_passes(coupling, coeffs, u_a, u_b):
    gain, size, b_sum = coeffs
    masks = plane_masks(1)

    def sea(w):
        return gain[w, FIELDS]

    def sweep_into(target):
        def emit(w, f, u, near, off):
            target[w, f] = (0.2 * u + b_sum[w, f]) + gain[w, f] * (near - off)

        return emit

    def residual(w, f, u, near, off):
        u_b[w, f] = ((b_sum[w, f] - OMEGA * u) + gain[w, f] * (near - off)) * size[w, f]

    def a_to_b(start, stop):
        stencil(start, stop, u_a, sea, coupling, masks, 1, sweep_into(u_b))

    def b_to_a(start, stop):
        stencil(start, stop, u_b, sea, coupling, masks, 1, sweep_into(u_a))

    def rest(start, stop):
        stencil(start, stop, u_a, sea, coupling, masks, 1, residual)

    return a_to_b, b_to_a, rest


def inner_passes(coupling, coeffs, u_a, u_b):
    for turn, one in enumerate(fine_passes(coupling, coeffs, u_a, u_b)):
        one(BASE + 1 + turn, BASE + OWN - 1 - turn)


def chip_passes(coupling, coeffs, u_a, u_b):
    for turn, one in enumerate(fine_passes(coupling, coeffs, u_a, u_b)):
        one(BASE + OWN - 1 - turn, BASE + OWN + HALO - 1 - turn)


def solve(coupling, coeffs, gain_c, u_a, u_b, e_a, e_b, rhs_c):
    gain = coeffs[0]
    passes = fine_passes(coupling, coeffs, u_a, u_b)
    for turn, one in enumerate(passes):
        one(BASE - HALO + 1 + turn, BASE + 1 + turn)

    places = Places()

    def restrict(c, carry):
        s = gain_c[c, 1]
        mean = places.gather([u_b[2 * c, f] + u_b[2 * c + 1, f] for f in range(FIELDS)]) * 0.125
        first = (gain_c[c, 0] + (1.0 - s) * OMEGA) * (s * mean)
        rhs_c[c, 0] = first
        e_a[c, 0] = first
        return carry

    lax.fori_loop(2, 20, restrict, 0, unroll=UNROLL[0])
    coarse_stencil(3, 19, e_a, e_b, gain_c, rhs_c, coupling, places)
    coarse_stencil(4, 18, e_b, e_a, gain_c, rhs_c, coupling, places)
    coarse_stencil(5, 17, e_a, e_b, gain_c, rhs_c, coupling, places)

    def correct(c, carry):
        e = places.spread(e_b[c, 0])
        for w in (2 * c, 2 * c + 1):
            for f in range(FIELDS):
                u_a[w, f] = u_a[w, f] + gain[w, FIELDS] * e[f]
        return carry

    lax.fori_loop(5, 17, correct, 0, unroll=UNROLL[1])
    passes[0](12, 32)
    passes[1](13, 31)
    passes[0](14, 30)


def each_plane(ref, count, place, visit):
    def body(i, carry):
        visit(place(i), ref, i)
        return carry

    lax.fori_loop(0, count, body, 0, unroll=UNROLL[2])


def own_place(i):
    return BASE + i


def chip_place(i):
    return BASE + OWN + i


def next_place(i):
    return BASE - 1 - i


def read_coupling(coupling_ref):
    return [[coupling_ref[f, g] for g in range(FIELDS)] for f in range(FIELDS)]


def fine_coefficients(table, coupling, coeffs, u_a, kappas):
    gain, size, b_sum = coeffs

    def visit(w, ref, at):
        s = ref[at, 4]
        kind = ref[at, 5]
        gain[w, FIELDS] = s
        hits = [kind == float(c) for c in range(CLASSES)]
        for f in range(FIELDS):
            kappa = jnp.zeros_like(s)
            for c in range(CLASSES):
                kappa = jnp.where(hits[c], table[c][f], kappa)
            diag = s * (kappa + (coupling[f][f] + 6.0)) + (1.0 - s)
            rate = OMEGA / diag
            first = rate * (s * ref[at, f])
            gain[w, f] = s * rate
            size[w, f] = diag * (1.0 / OMEGA)
            b_sum[w, f] = first
            u_a[w, f] = first
            kappas[w, f] = kappa

    return visit


def coarse_coefficients(coupling, gain, gain_c, kappas):
    places = Places()
    own = places.choose([jnp.full((8, 128), coupling[f][f] + 1.5, F32) for f in range(FIELDS)])

    def visit(c, carry):
        s = jnp.minimum(places.total(gain[2 * c, FIELDS] + gain[2 * c + 1, FIELDS]), 1.0)
        kappa = places.gather([kappas[2 * c, f] + kappas[2 * c + 1, f] for f in range(FIELDS)]) * 0.125
        diag = s * (kappa + own) + (1.0 - s)
        gain_c[c, 0] = s * (OMEGA / diag)
        gain_c[c, 1] = s
        return carry

    return visit


def read_table(table_ref):
    return [[table_ref[c, f] for f in range(FIELDS)] for c in range(CLASSES)]


def first_part(table_ref, coupling_ref, ref, place, cells, coeffs, gain_c, u_a, kappas):
    coupling = read_coupling(coupling_ref)
    each_plane(ref, ref.shape[0], place, fine_coefficients(read_table(table_ref), coupling, coeffs, u_a, kappas))
    visit = coarse_coefficients(coupling, coeffs[0], gain_c, kappas)
    start, stop = cells
    lax.fori_loop(start, stop, visit, 0, unroll=UNROLL[3])
    return coupling


def inner_first_kernel(table_ref, coupling_ref, own_ref, gain, size, b_sum, gain_c, u_a, u_b):
    coeffs = (gain, size, b_sum)
    coupling = first_part(table_ref, coupling_ref, own_ref, own_place, (7, 15), coeffs, gain_c, u_a, u_b)
    inner_passes(coupling, coeffs, u_a, u_b)


def chip_first_kernel(table_ref, coupling_ref, chip_ref, *refs):
    gain, size, b_sum, gain_c, u_a, u_b, kappas = refs[6:]
    coeffs = (gain, size, b_sum)
    coupling = first_part(table_ref, coupling_ref, chip_ref, chip_place, (15, 20), coeffs, gain_c, u_a, kappas)
    chip_passes(coupling, coeffs, u_a, u_b)


def first_kernel(table_ref, coupling_ref, next_ref, *refs):
    gain, size, b_sum, gain_c, u_a, u_b, out_ref, to_chip, to_next, e_a, e_b, rhs_c, kappas = refs[6:]
    coeffs = (gain, size, b_sum)
    coupling = first_part(table_ref, coupling_ref, next_ref, next_place, (2, 7), coeffs, gain_c, u_a, kappas)
    solve(coupling, coeffs, gain_c, u_a, u_b, e_a, e_b, rhs_c)
    out_ref[...] = u_b[BASE : BASE + OWN]
    share(out_ref, to_chip, to_next)


def second_start(coeffs, u_a):
    gain, _, b_sum = coeffs

    def visit(w, ref, at):
        land = (1.0 - gain[w, FIELDS]) * OMEGA
        for f in range(FIELDS):
            first = (gain[w, f] + land) * ref[at, f]
            b_sum[w, f] = first
            u_a[w, f] = first

    return visit


def send_rows(odd, kind, plane_of, out_ref):
    lane = lanes()
    place = (lane % 8) * 16 + (lane // 8) % 8
    lower = lane < 64
    for o in range(OWN):
        for q in range(2):
            pair = [plane_of(local(odd, o), 2 * q + h) for h in range(2)]
            for d in range(2):
                index = place + 8 * d
                rows = jnp.where(lower, pick(pair[0], index), pick(pair[1], index))
                out_ref[pl.ds(d * 512 + kind * 32 + q * 16 + o, 8, stride=64), :] = rows


def inner_second_kernel(me_ref, coupling_ref, own_ref, gain, size, b_sum, u_a, u_b, out_ref):
    coeffs = (gain, size, b_sum)
    each_plane(own_ref, OWN, own_place, second_start(coeffs, u_a))
    inner_passes(read_coupling(coupling_ref), coeffs, u_a, u_b)
    send_rows(is_odd(me_ref[0]), 0, lambda at, f: own_ref[at, f], out_ref)


def chip_second_kernel(coupling_ref, chip_ref, gain, size, *refs):
    b_sum, u_a, u_b = refs[3:]
    coeffs = (gain, size, b_sum)
    each_plane(chip_ref, HALO, chip_place, second_start(coeffs, u_a))
    chip_passes(read_coupling(coupling_ref), coeffs, u_a, u_b)


def second_kernel(me_ref, coupling_ref, next_ref, gain, size, gain_c, *refs):
    b_sum, u_a, u_b, out_ref, e_a, e_b, rhs_c = refs[4:]
    coeffs = (gain, size, b_sum)
    each_plane(next_ref, HALO, next_place, second_start(coeffs, u_a))
    solve(read_coupling(coupling_ref), coeffs, gain_c, u_a, u_b, e_a, e_b, rhs_c)
    send_rows(is_odd(me_ref[0]), 1, lambda at, f: u_b[BASE + at, f], out_ref)


def finish_kernel(me_ref, in_ref, first_ref, second_ref, turned):
    block = lax.div(me_ref[0], 16)
    for k, out_ref in enumerate((first_ref, second_ref)):
        for q in range(2):
            for chunk in range(16):
                at = pl.multiple_of(block_rank(block, chunk) * 16, 16)
                turned[2 * k + q, pl.ds(at, 16), :] = in_ref[chunk, k * 32 + q * 16 : k * 32 + q * 16 + 16, :]
            for half in range(2):
                pair = turned[2 * k + q, half * 128 : half * 128 + 128, :].T
                for h in range(2):
                    out_ref[2 * q + h, :, :, half * 128 : half * 128 + 128] = pair[64 * h : 64 * h + 64].reshape(8, 8, 128)


def planes(count, kinds=FIELDS):
    return jax.ShapeDtypeStruct((count, kinds, 8, 128), F32)


def scratch(count, kinds=FIELDS):
    return pltpu.VMEM((count, kinds, 8, 128), F32)


def per_device(source, sea_mask, classes, kappa_table, coupling):
    me = lax.axis_index(AXES).astype(jnp.int32).reshape(1)
    chips = [(device_of(g ^ 1), device_of(g)) for g in range(256)]
    nexts = [(device_of(((g + 1) ^ 1) - 1), device_of(g)) for g in range(256)]

    def trade(to_chip, to_next):
        from_next = lax.ppermute(to_next, AXES, nexts)
        return lax.ppermute(to_chip, AXES, chips), from_next

    sent = pl.pallas_call(
        pack_kernel,
        out_shape=jax.ShapeDtypeStruct((16, 48, 128), F32),
        in_specs=smem(1) + vmem(1),
        out_specs=vmem(1)[0],
        scratch_shapes=[pltpu.VMEM((3, 256, 128), F32)],
        compiler_params=params(),
        name="pack",
    )(me, jnp.concatenate([x.astype(F32).reshape(-1, 256) for x in (source, sea_mask, classes)]))
    got = lax.all_to_all(sent, ("dep", "lat"), 0, 0, tiled=False)
    def call(kernel, given, numbers, state, more, work, name):
        return pl.pallas_call(
            kernel,
            out_shape=tuple(state) + tuple(more),
            in_specs=smem(numbers) + vmem(len(given) - numbers + len(state)),
            out_specs=tuple(vmem(len(state) + len(more))),
            scratch_shapes=work,
            input_output_aliases={len(given) + i: i for i in range(len(state))},
            compiler_params=params(),
            cost_estimate=pl.CostEstimate(flops=40_000_000, bytes_accessed=8_000_000, transcendentals=0),
            name=name,
        )(*given, *state)

    halo = [planes(HALO), planes(HALO)]
    coarse = [scratch(COARSE_WIDE, 1)] * 3
    rows = jax.ShapeDtypeStruct((1024, 128), F32)
    given = [me, got.reshape(768, 128)]
    own, to_chip, to_next = call(unpack_kernel, given, 1, [], [planes(OWN, 6), planes(HALO, 6), planes(HALO, 6)], [], "unpack")
    mate, beyond = trade(to_chip, to_next)

    fresh = [planes(WIDE, 5), planes(WIDE), planes(WIDE), planes(COARSE_WIDE, 2), planes(WIDE), planes(WIDE)]
    numbers = [kappa_table, coupling]
    state = call(inner_first_kernel, numbers + [own], 2, [], fresh, [], "inner_first")
    state = call(chip_first_kernel, numbers + [mate], 2, state, [], [scratch(WIDE)], "chip_first")
    more = [planes(OWN)] + halo
    state = call(first_kernel, numbers + [beyond], 2, state, more, coarse + [scratch(WIDE)], "first")
    gain, size, _, gain_c, _, _, first, to_chip, to_next = state
    mate, beyond = trade(to_chip, to_next)

    fresh = [planes(WIDE), planes(WIDE), planes(WIDE), rows]
    state = call(inner_second_kernel, [me, coupling, first, gain, size], 2, [], fresh, [], "inner_second")
    sent = state[3]
    state = call(chip_second_kernel, [coupling, mate, gain, size], 1, state[:3], [], [], "chip_second")
    state = call(second_kernel, [me, coupling, beyond, gain, size, gain_c], 2, list(state) + [sent], [], coarse, "second")
    sent = state[3]
    got = lax.all_to_all(sent.reshape(16, 64, 128), ("dep", "lat"), 0, 0, tiled=False)
    out = jax.ShapeDtypeStruct((FIELDS, 8, 8, 256), F32)
    return pl.pallas_call(
        finish_kernel,
        out_shape=(out, out),
        in_specs=smem(1) + vmem(1),
        out_specs=tuple(vmem(2)),
        scratch_shapes=[pltpu.VMEM((4, 256, 128), F32)],
        compiler_params=params(),
        name="finish",
    )(me, got)


def solution(mesh):
    return jax.shard_map(
        per_device,
        mesh=mesh,
        in_specs=(
            P(None, "dep", "lat", "lon"),
            P("dep", "lat", "lon"),
            P("dep", "lat", "lon"),
            P(),
            P(),
        ),
        out_specs=(P(None, "dep", "lat", "lon"), P(None, "dep", "lat", "lon")),
        check_vma=False,
    )
```

```python
import functools

import jax
import jax.numpy as jnp
from jax import lax
from jax.experimental import pallas as pl
from jax.experimental.pallas import tpu as pltpu
from jax.sharding import PartitionSpec as P


FIELDS = 4
CLASSES = 8
OMEGA = 0.8
OWN = 16
HALO = 13
BASE = 14
WIDE = OWN + 2 * BASE
COARSE_WIDE = WIDE // 2
UNROLL = (9, 12, 13, 4)
AXES = ("lon", "lat", "dep")
F32 = jnp.float32
VMEM_LIMIT = 48 * 1024 * 1024


PATHS = (
    ((1, 1), (2, 1), (3, 1), (0, 1), (0, 0), (3, 0), (2, 0), (1, 0)),
    ((1, 1), (2, 1), (3, 1), (0, 1), (0, 0), (3, 0), (2, 0), (1, 0)),
)


def spots(path):
    return [(2 * x + core, dep) for x, dep in path for core in ((1, 0) if dep else (0, 1))]


PLACES = [spots(path) for path in PATHS]


def device_of(slab):
    block, rank = divmod(slab % 256, 16)
    lat, dep = PLACES[block // 8][rank if block % 2 == 0 else 15 - rank]
    return (block * 8 + lat) * 2 + dep


def params():
    return pltpu.CompilerParams(vmem_limit_bytes=VMEM_LIMIT)


def vmem(count):
    return [pl.BlockSpec(memory_space=pltpu.VMEM)] * count


def smem(count):
    return [pl.BlockSpec(memory_space=pltpu.SMEM)] * count


def is_odd(me):
    block, lat, dep = lax.div(me, 16), lax.rem(lax.div(me, 2), 8), lax.rem(me, 2)
    return lax.rem(block + lat + dep, 2)


def block_rank(block, chunk):
    low, high = (places.index((chunk % 8, chunk // 8)) for places in PLACES)
    rank = low if low == high else jnp.where(block < 8, low, high)
    odd = lax.rem(block, 2)
    return rank + odd * (15 - 2 * rank)


def pack_kernel(me_ref, rows_ref, out_ref, turned):
    block = lax.div(me_ref[0], 16)
    for q in range(3):
        for half in range(2):
            tile = rows_ref[128 * q : 128 * q + 128, half * 128 : half * 128 + 128]
            turned[q, half * 128 : half * 128 + 128, :] = tile.T
    for chunk in range(16):
        at = pl.multiple_of(block_rank(block, chunk) * 16, 16)
        for q in range(3):
            out_ref[chunk, q * 16 : q * 16 + 16, :] = turned[q, pl.ds(at, 16), :]


def lanes():
    return lax.broadcasted_iota(jnp.int32, (8, 128), 1)


def pick(value, index):
    return jnp.take_along_axis(value, index, axis=1, mode="promise_in_bounds")


def share(own_ref, to_chip, to_next):
    for i in range(HALO):
        to_chip[i] = own_ref[OWN - 1 - i]
        to_next[i] = own_ref[i]


def local(odd, o):
    return o + odd * (OWN - 1 - 2 * o)


def unpack_kernel(me_ref, in_ref, own_ref, to_chip, to_next):
    lane = lanes()
    row, depth = lane // 16, lane % 16
    place = (depth % 8) * 8 + row
    upper = depth >= 8
    odd = is_odd(me_ref[0])
    for o in range(OWN):
        for q in range(3):
            parts = [in_ref[pl.ds(d * 384 + q * 16 + o, 8, stride=48), :] for d in range(2)]
            for half in range(2):
                index = place + 64 * half
                own_ref[local(odd, o), 2 * q + half] = jnp.where(upper, pick(parts[1], index), pick(parts[0], index))
    share(own_ref, to_chip, to_next)


def plane_masks(step):
    lane = lanes()
    row = lax.broadcasted_iota(jnp.int32, (8, 128), 0)
    depth = lane % 16
    return (
        lane < 16 * step,
        row == 7,
        lane >= 128 - 16 * step,
        row == 0,
        jnp.where(depth >= 16 - step, 0.0, 1.0).astype(F32),
        jnp.where(depth < step, 0.0, 1.0).astype(F32),
    )


def plane_near(v, masks, step):
    first, top, last, bottom, keep_up, keep_down = masks
    zero = jnp.zeros_like(v)
    above = jnp.where(first, jnp.where(top, zero, pltpu.roll(v, 7, 0)), v)
    below = jnp.where(last, jnp.where(bottom, zero, pltpu.roll(v, 1, 0)), v)
    total = pltpu.roll(above, 128 - 16 * step, 1) + pltpu.roll(below, 16 * step, 1)
    return total + (pltpu.roll(v, 128 - step, 1) * keep_up + pltpu.roll(v, step, 1) * keep_down)


def stencil(start, stop, u_ref, sea, coupling, masks, step, emit):
    def load(w):
        u = [u_ref[w, f] for f in range(FIELDS)]
        s = sea(w)
        return u, [s * x for x in u]

    _, before = load(start - 1)
    u, v = load(start)
    for w in range(start, stop):
        u_next, after = load(w + 1)
        for f in range(FIELDS):
            near = (before[f] + after[f]) + plane_near(v[f], masks, step)
            others = [coupling[f][g] * u[g] for g in range(FIELDS) if g != f]
            emit(w, f, u[f], near, others[0] + others[1] + others[2])
        before, u, v = v, u_next, after


class Places:
    def __init__(self):
        lane = lanes()
        self.swaps = [jnp.bitwise_xor(lane, x) for x in (1, 16, 17)]
        self.even_depth = lane % 2 == 0
        self.even_lat = (lane // 16) % 2 == 0

    def turn(self, value, x):
        return pick(value, self.swaps[x - 1]) if x else value

    def choose(self, values):
        low = jnp.where(self.even_depth, values[0], values[1])
        return jnp.where(self.even_lat, low, jnp.where(self.even_depth, values[2], values[3]))

    def gather(self, t):
        pairs = []
        for x, y in ((t[0], t[1]), (t[2], t[3])):
            pairs.append(jnp.where(self.even_depth, x, y) + self.turn(jnp.where(self.even_depth, y, x), 1))
        x, y = pairs
        return jnp.where(self.even_lat, x, y) + self.turn(jnp.where(self.even_lat, y, x), 2)

    def total(self, t):
        t = t + self.turn(t, 1)
        return t + self.turn(t, 2)

    def spread(self, packed):
        turned = [self.turn(packed, x) for x in range(4)]
        return [self.choose([turned[p ^ f] for p in range(4)]) for f in range(FIELDS)]


def coarse_stencil(start, stop, e_ref, target, gain_c, rhs_c, coupling, places):
    masks = plane_masks(2)
    mix = [places.choose([jnp.full((8, 128), coupling[f][f ^ x], F32) for f in range(FIELDS)]) for x in range(1, 4)]

    def load(c):
        e = e_ref[c, 0]
        return e, gain_c[c, 1] * e

    _, before = load(start - 1)
    e, v = load(start)
    for c in range(start, stop):
        e_next, after = load(c + 1)
        near = (before + after) + plane_near(v, masks, 2)
        off = mix[0] * places.turn(e, 1) + mix[1] * places.turn(e, 2) + mix[2] * places.turn(e, 3)
        target[c, 0] = (0.2 * e + rhs_c[c, 0]) + gain_c[c, 0] * (0.25 * near - off)
        before, e, v = v, e_next, after


def fine_passes(coupling, coeffs, u_a, u_b):
    gain, size, b_sum = coeffs
    masks = plane_masks(1)

    def sea(w):
        return gain[w, FIELDS]

    def sweep_into(target):
        def emit(w, f, u, near, off):
            target[w, f] = (0.2 * u + b_sum[w, f]) + gain[w, f] * (near - off)

        return emit

    def residual(w, f, u, near, off):
        u_b[w, f] = ((b_sum[w, f] - OMEGA * u) + gain[w, f] * (near - off)) * size[w, f]

    def a_to_b(start, stop):
        stencil(start, stop, u_a, sea, coupling, masks, 1, sweep_into(u_b))

    def b_to_a(start, stop):
        stencil(start, stop, u_b, sea, coupling, masks, 1, sweep_into(u_a))

    def rest(start, stop):
        stencil(start, stop, u_a, sea, coupling, masks, 1, residual)

    return a_to_b, b_to_a, rest


def inner_passes(coupling, coeffs, u_a, u_b):
    for turn, one in enumerate(fine_passes(coupling, coeffs, u_a, u_b)):
        one(BASE + 1 + turn, BASE + OWN - 1 - turn)


def chip_passes(coupling, coeffs, u_a, u_b):
    for turn, one in enumerate(fine_passes(coupling, coeffs, u_a, u_b)):
        one(BASE + OWN - 1 - turn, BASE + OWN + HALO - 1 - turn)


def solve(coupling, coeffs, gain_c, u_a, u_b, e_a, e_b, rhs_c):
    gain = coeffs[0]
    passes = fine_passes(coupling, coeffs, u_a, u_b)
    for turn, one in enumerate(passes):
        one(BASE - HALO + 1 + turn, BASE + 1 + turn)

    places = Places()

    def restrict(c, carry):
        s = gain_c[c, 1]
        mean = places.gather([u_b[2 * c, f] + u_b[2 * c + 1, f] for f in range(FIELDS)]) * 0.125
        first = (gain_c[c, 0] + (1.0 - s) * OMEGA) * (s * mean)
        rhs_c[c, 0] = first
        e_a[c, 0] = first
        return carry

    lax.fori_loop(2, 20, restrict, 0, unroll=UNROLL[0])
    coarse_stencil(3, 19, e_a, e_b, gain_c, rhs_c, coupling, places)
    coarse_stencil(4, 18, e_b, e_a, gain_c, rhs_c, coupling, places)
    coarse_stencil(5, 17, e_a, e_b, gain_c, rhs_c, coupling, places)

    def correct(c, carry):
        e = places.spread(e_b[c, 0])
        for w in (2 * c, 2 * c + 1):
            for f in range(FIELDS):
                u_a[w, f] = u_a[w, f] + gain[w, FIELDS] * e[f]
        return carry

    lax.fori_loop(5, 17, correct, 0, unroll=UNROLL[1])
    passes[0](12, 32)
    passes[1](13, 31)
    passes[0](14, 30)


def each_plane(ref, count, place, visit):
    def body(i, carry):
        visit(place(i), ref, i)
        return carry

    lax.fori_loop(0, count, body, 0, unroll=UNROLL[2])


def own_place(i):
    return BASE + i


def chip_place(i):
    return BASE + OWN + i


def next_place(i):
    return BASE - 1 - i


def read_coupling(coupling_ref):
    return [[coupling_ref[f, g] for g in range(FIELDS)] for f in range(FIELDS)]


def fine_coefficients(table, coupling, coeffs, u_a, kappas):
    gain, size, b_sum = coeffs

    def visit(w, ref, at):
        s = ref[at, 4]
        kind = ref[at, 5]
        gain[w, FIELDS] = s
        hits = [kind == float(c) for c in range(CLASSES)]
        for f in range(FIELDS):
            kappa = jnp.zeros_like(s)
            for c in range(CLASSES):
                kappa = jnp.where(hits[c], table[c][f], kappa)
            diag = s * (kappa + (coupling[f][f] + 6.0)) + (1.0 - s)
            rate = OMEGA / diag
            first = rate * (s * ref[at, f])
            gain[w, f] = s * rate
            size[w, f] = diag * (1.0 / OMEGA)
            b_sum[w, f] = first
            u_a[w, f] = first
            kappas[w, f] = kappa

    return visit


def coarse_coefficients(coupling, gain, gain_c, kappas):
    places = Places()
    own = places.choose([jnp.full((8, 128), coupling[f][f] + 1.5, F32) for f in range(FIELDS)])

    def visit(c, carry):
        s = jnp.minimum(places.total(gain[2 * c, FIELDS] + gain[2 * c + 1, FIELDS]), 1.0)
        kappa = places.gather([kappas[2 * c, f] + kappas[2 * c + 1, f] for f in range(FIELDS)]) * 0.125
        diag = s * (kappa + own) + (1.0 - s)
        gain_c[c, 0] = s * (OMEGA / diag)
        gain_c[c, 1] = s
        return carry

    return visit


def read_table(table_ref):
    return [[table_ref[c, f] for f in range(FIELDS)] for c in range(CLASSES)]


def first_part(table_ref, coupling_ref, ref, place, cells, coeffs, gain_c, u_a, kappas):
    coupling = read_coupling(coupling_ref)
    each_plane(ref, ref.shape[0], place, fine_coefficients(read_table(table_ref), coupling, coeffs, u_a, kappas))
    visit = coarse_coefficients(coupling, coeffs[0], gain_c, kappas)
    start, stop = cells
    lax.fori_loop(start, stop, visit, 0, unroll=UNROLL[3])
    return coupling


def inner_first_kernel(table_ref, coupling_ref, own_ref, gain, size, b_sum, gain_c, u_a, u_b):
    coeffs = (gain, size, b_sum)
    coupling = first_part(table_ref, coupling_ref, own_ref, own_place, (7, 15), coeffs, gain_c, u_a, u_b)
    inner_passes(coupling, coeffs, u_a, u_b)


def chip_first_kernel(table_ref, coupling_ref, chip_ref, *refs):
    gain, size, b_sum, gain_c, u_a, u_b, kappas = refs[6:]
    coeffs = (gain, size, b_sum)
    coupling = first_part(table_ref, coupling_ref, chip_ref, chip_place, (15, 20), coeffs, gain_c, u_a, kappas)
    chip_passes(coupling, coeffs, u_a, u_b)


def first_kernel(table_ref, coupling_ref, next_ref, *refs):
    gain, size, b_sum, gain_c, u_a, u_b, out_ref, to_chip, to_next, e_a, e_b, rhs_c, kappas = refs[6:]
    coeffs = (gain, size, b_sum)
    coupling = first_part(table_ref, coupling_ref, next_ref, next_place, (2, 7), coeffs, gain_c, u_a, kappas)
    solve(coupling, coeffs, gain_c, u_a, u_b, e_a, e_b, rhs_c)
    out_ref[...] = u_b[BASE : BASE + OWN]
    share(out_ref, to_chip, to_next)


def second_start(coeffs, u_a):
    gain, _, b_sum = coeffs

    def visit(w, ref, at):
        land = (1.0 - gain[w, FIELDS]) * OMEGA
        for f in range(FIELDS):
            first = (gain[w, f] + land) * ref[at, f]
            b_sum[w, f] = first
            u_a[w, f] = first

    return visit


def send_rows(odd, kind, plane_of, out_ref):
    lane = lanes()
    place = (lane % 8) * 16 + (lane // 8) % 8
    lower = lane < 64
    for o in range(OWN):
        for q in range(2):
            pair = [plane_of(local(odd, o), 2 * q + h) for h in range(2)]
            for d in range(2):
                index = place + 8 * d
                rows = jnp.where(lower, pick(pair[0], index), pick(pair[1], index))
                out_ref[pl.ds(d * 512 + kind * 32 + q * 16 + o, 8, stride=64), :] = rows


def inner_second_kernel(me_ref, coupling_ref, own_ref, gain, size, b_sum, u_a, u_b, out_ref):
    coeffs = (gain, size, b_sum)
    each_plane(own_ref, OWN, own_place, second_start(coeffs, u_a))
    inner_passes(read_coupling(coupling_ref), coeffs, u_a, u_b)
    send_rows(is_odd(me_ref[0]), 0, lambda at, f: own_ref[at, f], out_ref)


def chip_second_kernel(coupling_ref, chip_ref, gain, size, *refs):
    b_sum, u_a, u_b = refs[3:]
    coeffs = (gain, size, b_sum)
    each_plane(chip_ref, HALO, chip_place, second_start(coeffs, u_a))
    chip_passes(read_coupling(coupling_ref), coeffs, u_a, u_b)


def second_kernel(me_ref, coupling_ref, next_ref, gain, size, gain_c, *refs):
    b_sum, u_a, u_b, out_ref, e_a, e_b, rhs_c = refs[4:]
    coeffs = (gain, size, b_sum)
    each_plane(next_ref, HALO, next_place, second_start(coeffs, u_a))
    solve(read_coupling(coupling_ref), coeffs, gain_c, u_a, u_b, e_a, e_b, rhs_c)
    send_rows(is_odd(me_ref[0]), 1, lambda at, f: u_b[BASE + at, f], out_ref)


def finish_kernel(me_ref, in_ref, first_ref, second_ref, turned):
    block = lax.div(me_ref[0], 16)
    for k, out_ref in enumerate((first_ref, second_ref)):
        for q in range(2):
            for chunk in range(16):
                at = pl.multiple_of(block_rank(block, chunk) * 16, 16)
                turned[2 * k + q, pl.ds(at, 16), :] = in_ref[chunk, k * 32 + q * 16 : k * 32 + q * 16 + 16, :]
            for half in range(2):
                pair = turned[2 * k + q, half * 128 : half * 128 + 128, :].T
                for h in range(2):
                    out_ref[2 * q + h, :, :, half * 128 : half * 128 + 128] = pair[64 * h : 64 * h + 64].reshape(8, 8, 128)


def planes(count, kinds=FIELDS):
    return jax.ShapeDtypeStruct((count, kinds, 8, 128), F32)


def scratch(count, kinds=FIELDS):
    return pltpu.VMEM((count, kinds, 8, 128), F32)


def per_device(source, sea_mask, classes, kappa_table, coupling):
    me = lax.axis_index(AXES).astype(jnp.int32).reshape(1)
    chips = [(device_of(g ^ 1), device_of(g)) for g in range(256)]
    nexts = [(device_of(((g + 1) ^ 1) - 1), device_of(g)) for g in range(256)]

    def trade(to_chip, to_next):
        from_next = lax.ppermute(to_next, AXES, nexts)
        return lax.ppermute(to_chip, AXES, chips), from_next

    sent = pl.pallas_call(
        pack_kernel,
        out_shape=jax.ShapeDtypeStruct((16, 48, 128), F32),
        in_specs=smem(1) + vmem(1),
        out_specs=vmem(1)[0],
        scratch_shapes=[pltpu.VMEM((3, 256, 128), F32)],
        compiler_params=params(),
        name="pack",
    )(me, jnp.concatenate([x.astype(F32).reshape(-1, 256) for x in (source, sea_mask, classes)]))
    got = lax.all_to_all(sent, ("dep", "lat"), 0, 0, tiled=False)
    def call(kernel, given, numbers, state, more, work, name):
        return pl.pallas_call(
            kernel,
            out_shape=tuple(state) + tuple(more),
            in_specs=smem(numbers) + vmem(len(given) - numbers + len(state)),
            out_specs=tuple(vmem(len(state) + len(more))),
            scratch_shapes=work,
            input_output_aliases={len(given) + i: i for i in range(len(state))},
            compiler_params=params(),
            cost_estimate=pl.CostEstimate(flops=40_000_000, bytes_accessed=8_000_000, transcendentals=0),
            name=name,
        )(*given, *state)

    halo = [planes(HALO), planes(HALO)]
    coarse = [scratch(COARSE_WIDE, 1)] * 3
    rows = jax.ShapeDtypeStruct((1024, 128), F32)
    given = [me, got.reshape(768, 128)]
    own, to_chip, to_next = call(unpack_kernel, given, 1, [], [planes(OWN, 6), planes(HALO, 6), planes(HALO, 6)], [], "unpack")
    mate, beyond = trade(to_chip, to_next)

    fresh = [planes(WIDE, 5), planes(WIDE), planes(WIDE), planes(COARSE_WIDE, 2), planes(WIDE), planes(WIDE)]
    numbers = [kappa_table, coupling]
    state = call(inner_first_kernel, numbers + [own], 2, [], fresh, [], "inner_first")
    state = call(chip_first_kernel, numbers + [mate], 2, state, [], [scratch(WIDE)], "chip_first")
    more = [planes(OWN)] + halo
    state = call(first_kernel, numbers + [beyond], 2, state, more, coarse + [scratch(WIDE)], "first")
    gain, size, _, gain_c, _, _, first, to_chip, to_next = state
    mate, beyond = trade(to_chip, to_next)

    fresh = [planes(WIDE), planes(WIDE), planes(WIDE), rows]
    state = call(inner_second_kernel, [me, coupling, first, gain, size], 2, [], fresh, [], "inner_second")
    sent = state[3]
    state = call(chip_second_kernel, [coupling, mate, gain, size], 1, state[:3], [], [], "chip_second")
    state = call(second_kernel, [me, coupling, beyond, gain, size, gain_c], 2, list(state) + [sent], [], coarse, "second")
    sent = state[3]
    got = lax.all_to_all(sent.reshape(16, 64, 128), ("dep", "lat"), 0, 0, tiled=False)
    out = jax.ShapeDtypeStruct((FIELDS, 8, 8, 256), F32)
    return pl.pallas_call(
        finish_kernel,
        out_shape=(out, out),
        in_specs=smem(1) + vmem(1),
        out_specs=tuple(vmem(2)),
        scratch_shapes=[pltpu.VMEM((4, 256, 128), F32)],
        compiler_params=params(),
        name="finish",
    )(me, got)


def solution(mesh):
    return jax.shard_map(
        per_device,
        mesh=mesh,
        in_specs=(
            P(None, "dep", "lat", "lon"),
            P("dep", "lat", "lon"),
            P("dep", "lat", "lon"),
            P(),
            P(),
        ),
        out_specs=(P(None, "dep", "lat", "lon"), P(None, "dep", "lat", "lon")),
        check_vma=False,
    )
```

```python
import functools

import jax
import jax.numpy as jnp
from jax import lax
from jax.experimental import pallas as pl
from jax.experimental.pallas import tpu as pltpu
from jax.sharding import PartitionSpec as P


FIELDS = 4
CLASSES = 8
OMEGA = 0.8
OWN = 16
HALO = 13
BASE = 14
WIDE = OWN + 2 * BASE
COARSE_WIDE = WIDE // 2
UNROLL = (9, 12, 13, 4)
AXES = ("lon", "lat", "dep")
F32 = jnp.float32
VMEM_LIMIT = 48 * 1024 * 1024


PATHS = (
    ((1, 0), (2, 0), (3, 0), (0, 0), (0, 1), (3, 1), (2, 1), (1, 1)),
    ((1, 0), (2, 0), (3, 0), (0, 0), (0, 1), (3, 1), (2, 1), (1, 1)),
)


def spots(path):
    return [(2 * x + core, dep) for x, dep in path for core in ((0, 1) if dep else (1, 0))]


PLACES = [spots(path) for path in PATHS]


def device_of(slab):
    block, rank = divmod(slab % 256, 16)
    lat, dep = PLACES[block // 8][rank if block % 2 == 0 else 15 - rank]
    return (block * 8 + lat) * 2 + dep


def params():
    return pltpu.CompilerParams(vmem_limit_bytes=VMEM_LIMIT)


def vmem(count):
    return [pl.BlockSpec(memory_space=pltpu.VMEM)] * count


def smem(count):
    return [pl.BlockSpec(memory_space=pltpu.SMEM)] * count


def is_odd(me):
    block, lat, dep = lax.div(me, 16), lax.rem(lax.div(me, 2), 8), lax.rem(me, 2)
    return lax.rem(block + lat + dep + 1, 2)


def block_rank(block, chunk):
    low, high = (places.index((chunk % 8, chunk // 8)) for places in PLACES)
    rank = low if low == high else jnp.where(block < 8, low, high)
    odd = lax.rem(block, 2)
    return rank + odd * (15 - 2 * rank)


def pack_kernel(me_ref, rows_ref, out_ref, turned):
    block = lax.div(me_ref[0], 16)
    for q in range(3):
        for half in range(2):
            tile = rows_ref[128 * q : 128 * q + 128, half * 128 : half * 128 + 128]
            turned[q, half * 128 : half * 128 + 128, :] = tile.T
    for chunk in range(16):
        at = pl.multiple_of(block_rank(block, chunk) * 16, 16)
        for q in range(3):
            out_ref[chunk, q * 16 : q * 16 + 16, :] = turned[q, pl.ds(at, 16), :]


def lanes():
    return lax.broadcasted_iota(jnp.int32, (8, 128), 1)


def pick(value, index):
    return jnp.take_along_axis(value, index, axis=1, mode="promise_in_bounds")


def share(own_ref, to_chip, to_next):
    for i in range(HALO):
        to_chip[i] = own_ref[OWN - 1 - i]
        to_next[i] = own_ref[i]


def local(odd, o):
    return o + odd * (OWN - 1 - 2 * o)


def unpack_kernel(me_ref, in_ref, own_ref, to_chip, to_next):
    lane = lanes()
    row, depth = lane // 16, lane % 16
    place = (depth % 8) * 8 + row
    upper = depth >= 8
    odd = is_odd(me_ref[0])
    for o in range(OWN):
        for q in range(3):
            parts = [in_ref[pl.ds(d * 384 + q * 16 + o, 8, stride=48), :] for d in range(2)]
            for half in range(2):
                index = place + 64 * half
                own_ref[local(odd, o), 2 * q + half] = jnp.where(upper, pick(parts[1], index), pick(parts[0], index))
    share(own_ref, to_chip, to_next)


def plane_masks(step):
    lane = lanes()
    row = lax.broadcasted_iota(jnp.int32, (8, 128), 0)
    depth = lane % 16
    return (
        lane < 16 * step,
        row == 7,
        lane >= 128 - 16 * step,
        row == 0,
        jnp.where(depth >= 16 - step, 0.0, 1.0).astype(F32),
        jnp.where(depth < step, 0.0, 1.0).astype(F32),
    )


def plane_near(v, masks, step):
    first, top, last, bottom, keep_up, keep_down = masks
    zero = jnp.zeros_like(v)
    above = jnp.where(first, jnp.where(top, zero, pltpu.roll(v, 7, 0)), v)
    below = jnp.where(last, jnp.where(bottom, zero, pltpu.roll(v, 1, 0)), v)
    total = pltpu.roll(above, 128 - 16 * step, 1) + pltpu.roll(below, 16 * step, 1)
    return total + (pltpu.roll(v, 128 - step, 1) * keep_up + pltpu.roll(v, step, 1) * keep_down)


def stencil(start, stop, u_ref, sea, coupling, masks, step, emit):
    def load(w):
        u = [u_ref[w, f] for f in range(FIELDS)]
        s = sea(w)
        return u, [s * x for x in u]

    _, before = load(start - 1)
    u, v = load(start)
    for w in range(start, stop):
        u_next, after = load(w + 1)
        for f in range(FIELDS):
            near = (before[f] + after[f]) + plane_near(v[f], masks, step)
            others = [coupling[f][g] * u[g] for g in range(FIELDS) if g != f]
            emit(w, f, u[f], near, others[0] + others[1] + others[2])
        before, u, v = v, u_next, after


class Places:
    def __init__(self):
        lane = lanes()
        self.swaps = [jnp.bitwise_xor(lane, x) for x in (1, 16, 17)]
        self.even_depth = lane % 2 == 0
        self.even_lat = (lane // 16) % 2 == 0

    def turn(self, value, x):
        return pick(value, self.swaps[x - 1]) if x else value

    def choose(self, values):
        low = jnp.where(self.even_depth, values[0], values[1])
        return jnp.where(self.even_lat, low, jnp.where(self.even_depth, values[2], values[3]))

    def gather(self, t):
        pairs = []
        for x, y in ((t[0], t[1]), (t[2], t[3])):
            pairs.append(jnp.where(self.even_depth, x, y) + self.turn(jnp.where(self.even_depth, y, x), 1))
        x, y = pairs
        return jnp.where(self.even_lat, x, y) + self.turn(jnp.where(self.even_lat, y, x), 2)

    def total(self, t):
        t = t + self.turn(t, 1)
        return t + self.turn(t, 2)

    def spread(self, packed):
        turned = [self.turn(packed, x) for x in range(4)]
        return [self.choose([turned[p ^ f] for p in range(4)]) for f in range(FIELDS)]


def coarse_stencil(start, stop, e_ref, target, gain_c, rhs_c, coupling, places):
    masks = plane_masks(2)
    mix = [places.choose([jnp.full((8, 128), coupling[f][f ^ x], F32) for f in range(FIELDS)]) for x in range(1, 4)]

    def load(c):
        e = e_ref[c, 0]
        return e, gain_c[c, 1] * e

    _, before = load(start - 1)
    e, v = load(start)
    for c in range(start, stop):
        e_next, after = load(c + 1)
        near = (before + after) + plane_near(v, masks, 2)
        off = mix[0] * places.turn(e, 1) + mix[1] * places.turn(e, 2) + mix[2] * places.turn(e, 3)
        target[c, 0] = (0.2 * e + rhs_c[c, 0]) + gain_c[c, 0] * (0.25 * near - off)
        before, e, v = v, e_next, after


def fine_passes(coupling, coeffs, u_a, u_b):
    gain, size, b_sum = coeffs
    masks = plane_masks(1)

    def sea(w):
        return gain[w, FIELDS]

    def sweep_into(target):
        def emit(w, f, u, near, off):
            target[w, f] = (0.2 * u + b_sum[w, f]) + gain[w, f] * (near - off)

        return emit

    def residual(w, f, u, near, off):
        u_b[w, f] = ((b_sum[w, f] - OMEGA * u) + gain[w, f] * (near - off)) * size[w, f]

    def a_to_b(start, stop):
        stencil(start, stop, u_a, sea, coupling, masks, 1, sweep_into(u_b))

    def b_to_a(start, stop):
        stencil(start, stop, u_b, sea, coupling, masks, 1, sweep_into(u_a))

    def rest(start, stop):
        stencil(start, stop, u_a, sea, coupling, masks, 1, residual)

    return a_to_b, b_to_a, rest


def inner_passes(coupling, coeffs, u_a, u_b):
    for turn, one in enumerate(fine_passes(coupling, coeffs, u_a, u_b)):
        one(BASE + 1 + turn, BASE + OWN - 1 - turn)


def chip_passes(coupling, coeffs, u_a, u_b):
    for turn, one in enumerate(fine_passes(coupling, coeffs, u_a, u_b)):
        one(BASE + OWN - 1 - turn, BASE + OWN + HALO - 1 - turn)


def solve(coupling, coeffs, gain_c, u_a, u_b, e_a, e_b, rhs_c):
    gain = coeffs[0]
    passes = fine_passes(coupling, coeffs, u_a, u_b)
    for turn, one in enumerate(passes):
        one(BASE - HALO + 1 + turn, BASE + 1 + turn)

    places = Places()

    def restrict(c, carry):
        s = gain_c[c, 1]
        mean = places.gather([u_b[2 * c, f] + u_b[2 * c + 1, f] for f in range(FIELDS)]) * 0.125
        first = (gain_c[c, 0] + (1.0 - s) * OMEGA) * (s * mean)
        rhs_c[c, 0] = first
        e_a[c, 0] = first
        return carry

    lax.fori_loop(2, 20, restrict, 0, unroll=UNROLL[0])
    coarse_stencil(3, 19, e_a, e_b, gain_c, rhs_c, coupling, places)
    coarse_stencil(4, 18, e_b, e_a, gain_c, rhs_c, coupling, places)
    coarse_stencil(5, 17, e_a, e_b, gain_c, rhs_c, coupling, places)

    def correct(c, carry):
        e = places.spread(e_b[c, 0])
        for w in (2 * c, 2 * c + 1):
            for f in range(FIELDS):
                u_a[w, f] = u_a[w, f] + gain[w, FIELDS] * e[f]
        return carry

    lax.fori_loop(5, 17, correct, 0, unroll=UNROLL[1])
    passes[0](12, 32)
    passes[1](13, 31)
    passes[0](14, 30)


def each_plane(ref, count, place, visit):
    def body(i, carry):
        visit(place(i), ref, i)
        return carry

    lax.fori_loop(0, count, body, 0, unroll=UNROLL[2])


def own_place(i):
    return BASE + i


def chip_place(i):
    return BASE + OWN + i


def next_place(i):
    return BASE - 1 - i


def read_coupling(coupling_ref):
    return [[coupling_ref[f, g] for g in range(FIELDS)] for f in range(FIELDS)]


def fine_coefficients(table, coupling, coeffs, u_a, kappas):
    gain, size, b_sum = coeffs

    def visit(w, ref, at):
        s = ref[at, 4]
        kind = ref[at, 5]
        gain[w, FIELDS] = s
        hits = [kind == float(c) for c in range(CLASSES)]
        for f in range(FIELDS):
            kappa = jnp.zeros_like(s)
            for c in range(CLASSES):
                kappa = jnp.where(hits[c], table[c][f], kappa)
            diag = s * (kappa + (coupling[f][f] + 6.0)) + (1.0 - s)
            rate = OMEGA / diag
            first = rate * (s * ref[at, f])
            gain[w, f] = s * rate
            size[w, f] = diag * (1.0 / OMEGA)
            b_sum[w, f] = first
            u_a[w, f] = first
            kappas[w, f] = kappa

    return visit


def coarse_coefficients(coupling, gain, gain_c, kappas):
    places = Places()
    own = places.choose([jnp.full((8, 128), coupling[f][f] + 1.5, F32) for f in range(FIELDS)])

    def visit(c, carry):
        s = jnp.minimum(places.total(gain[2 * c, FIELDS] + gain[2 * c + 1, FIELDS]), 1.0)
        kappa = places.gather([kappas[2 * c, f] + kappas[2 * c + 1, f] for f in range(FIELDS)]) * 0.125
        diag = s * (kappa + own) + (1.0 - s)
        gain_c[c, 0] = s * (OMEGA / diag)
        gain_c[c, 1] = s
        return carry

    return visit


def read_table(table_ref):
    return [[table_ref[c, f] for f in range(FIELDS)] for c in range(CLASSES)]


def first_part(table_ref, coupling_ref, ref, place, cells, coeffs, gain_c, u_a, kappas):
    coupling = read_coupling(coupling_ref)
    each_plane(ref, ref.shape[0], place, fine_coefficients(read_table(table_ref), coupling, coeffs, u_a, kappas))
    visit = coarse_coefficients(coupling, coeffs[0], gain_c, kappas)
    start, stop = cells
    lax.fori_loop(start, stop, visit, 0, unroll=UNROLL[3])
    return coupling


def inner_first_kernel(table_ref, coupling_ref, own_ref, gain, size, b_sum, gain_c, u_a, u_b):
    coeffs = (gain, size, b_sum)
    coupling = first_part(table_ref, coupling_ref, own_ref, own_place, (7, 15), coeffs, gain_c, u_a, u_b)
    inner_passes(coupling, coeffs, u_a, u_b)


def chip_first_kernel(table_ref, coupling_ref, chip_ref, *refs):
    gain, size, b_sum, gain_c, u_a, u_b, kappas = refs[6:]
    coeffs = (gain, size, b_sum)
    coupling = first_part(table_ref, coupling_ref, chip_ref, chip_place, (15, 20), coeffs, gain_c, u_a, kappas)
    chip_passes(coupling, coeffs, u_a, u_b)


def first_kernel(table_ref, coupling_ref, next_ref, *refs):
    gain, size, b_sum, gain_c, u_a, u_b, out_ref, to_chip, to_next, e_a, e_b, rhs_c, kappas = refs[6:]
    coeffs = (gain, size, b_sum)
    coupling = first_part(table_ref, coupling_ref, next_ref, next_place, (2, 7), coeffs, gain_c, u_a, kappas)
    solve(coupling, coeffs, gain_c, u_a, u_b, e_a, e_b, rhs_c)
    out_ref[...] = u_b[BASE : BASE + OWN]
    share(out_ref, to_chip, to_next)


def second_start(coeffs, u_a):
    gain, _, b_sum = coeffs

    def visit(w, ref, at):
        land = (1.0 - gain[w, FIELDS]) * OMEGA
        for f in range(FIELDS):
            first = (gain[w, f] + land) * ref[at, f]
            b_sum[w, f] = first
            u_a[w, f] = first

    return visit


def send_rows(odd, kind, plane_of, out_ref):
    lane = lanes()
    place = (lane % 8) * 16 + (lane // 8) % 8
    lower = lane < 64
    for o in range(OWN):
        for q in range(2):
            pair = [plane_of(local(odd, o), 2 * q + h) for h in range(2)]
            for d in range(2):
                index = place + 8 * d
                rows = jnp.where(lower, pick(pair[0], index), pick(pair[1], index))
                out_ref[pl.ds(d * 512 + kind * 32 + q * 16 + o, 8, stride=64), :] = rows


def inner_second_kernel(me_ref, coupling_ref, own_ref, gain, size, b_sum, u_a, u_b, out_ref):
    coeffs = (gain, size, b_sum)
    each_plane(own_ref, OWN, own_place, second_start(coeffs, u_a))
    inner_passes(read_coupling(coupling_ref), coeffs, u_a, u_b)
    send_rows(is_odd(me_ref[0]), 0, lambda at, f: own_ref[at, f], out_ref)


def chip_second_kernel(coupling_ref, chip_ref, gain, size, *refs):
    b_sum, u_a, u_b = refs[3:]
    coeffs = (gain, size, b_sum)
    each_plane(chip_ref, HALO, chip_place, second_start(coeffs, u_a))
    chip_passes(read_coupling(coupling_ref), coeffs, u_a, u_b)


def second_kernel(me_ref, coupling_ref, next_ref, gain, size, gain_c, *refs):
    b_sum, u_a, u_b, out_ref, e_a, e_b, rhs_c = refs[4:]
    coeffs = (gain, size, b_sum)
    each_plane(next_ref, HALO, next_place, second_start(coeffs, u_a))
    solve(read_coupling(coupling_ref), coeffs, gain_c, u_a, u_b, e_a, e_b, rhs_c)
    send_rows(is_odd(me_ref[0]), 1, lambda at, f: u_b[BASE + at, f], out_ref)


def finish_kernel(me_ref, in_ref, first_ref, second_ref, turned):
    block = lax.div(me_ref[0], 16)
    for k, out_ref in enumerate((first_ref, second_ref)):
        for q in range(2):
            for chunk in range(16):
                at = pl.multiple_of(block_rank(block, chunk) * 16, 16)
                turned[2 * k + q, pl.ds(at, 16), :] = in_ref[chunk, k * 32 + q * 16 : k * 32 + q * 16 + 16, :]
            for half in range(2):
                pair = turned[2 * k + q, half * 128 : half * 128 + 128, :].T
                for h in range(2):
                    out_ref[2 * q + h, :, :, half * 128 : half * 128 + 128] = pair[64 * h : 64 * h + 64].reshape(8, 8, 128)


def planes(count, kinds=FIELDS):
    return jax.ShapeDtypeStruct((count, kinds, 8, 128), F32)


def scratch(count, kinds=FIELDS):
    return pltpu.VMEM((count, kinds, 8, 128), F32)


def per_device(source, sea_mask, classes, kappa_table, coupling):
    me = lax.axis_index(AXES).astype(jnp.int32).reshape(1)
    chips = [(device_of(g ^ 1), device_of(g)) for g in range(256)]
    nexts = [(device_of(((g + 1) ^ 1) - 1), device_of(g)) for g in range(256)]

    def trade(to_chip, to_next):
        from_chip = lax.ppermute(to_chip, AXES, chips)
        return from_chip, lax.ppermute(to_next, AXES, nexts)

    sent = pl.pallas_call(
        pack_kernel,
        out_shape=jax.ShapeDtypeStruct((16, 48, 128), F32),
        in_specs=smem(1) + vmem(1),
        out_specs=vmem(1)[0],
        scratch_shapes=[pltpu.VMEM((3, 256, 128), F32)],
        compiler_params=params(),
        name="pack",
    )(me, jnp.concatenate([x.astype(F32).reshape(-1, 256) for x in (source, sea_mask, classes)]))
    got = lax.all_to_all(sent, ("dep", "lat"), 0, 0, tiled=False)
    def call(kernel, given, numbers, state, more, work, name):
        return pl.pallas_call(
            kernel,
            out_shape=tuple(state) + tuple(more),
            in_specs=smem(numbers) + vmem(len(given) - numbers + len(state)),
            out_specs=tuple(vmem(len(state) + len(more))),
            scratch_shapes=work,
            input_output_aliases={len(given) + i: i for i in range(len(state))},
            compiler_params=params(),
            cost_estimate=pl.CostEstimate(flops=40_000_000, bytes_accessed=8_000_000, transcendentals=0),
            name=name,
        )(*given, *state)

    halo = [planes(HALO), planes(HALO)]
    coarse = [scratch(COARSE_WIDE, 1)] * 3
    rows = jax.ShapeDtypeStruct((1024, 128), F32)
    given = [me, got.reshape(768, 128)]
    own, to_chip, to_next = call(unpack_kernel, given, 1, [], [planes(OWN, 6), planes(HALO, 6), planes(HALO, 6)], [], "unpack")
    mate, beyond = trade(to_chip, to_next)

    fresh = [planes(WIDE, 5), planes(WIDE), planes(WIDE), planes(COARSE_WIDE, 2), planes(WIDE), planes(WIDE)]
    numbers = [kappa_table, coupling]
    state = call(inner_first_kernel, numbers + [own], 2, [], fresh, [], "inner_first")
    state = call(chip_first_kernel, numbers + [mate], 2, state, [], [scratch(WIDE)], "chip_first")
    more = [planes(OWN)] + halo
    state = call(first_kernel, numbers + [beyond], 2, state, more, coarse + [scratch(WIDE)], "first")
    gain, size, _, gain_c, _, _, first, to_chip, to_next = state
    mate, beyond = trade(to_chip, to_next)

    fresh = [planes(WIDE), planes(WIDE), planes(WIDE), rows]
    state = call(inner_second_kernel, [me, coupling, first, gain, size], 2, [], fresh, [], "inner_second")
    sent = state[3]
    state = call(chip_second_kernel, [coupling, mate, gain, size], 1, state[:3], [], [], "chip_second")
    state = call(second_kernel, [me, coupling, beyond, gain, size, gain_c], 2, list(state) + [sent], [], coarse, "second")
    sent = state[3]
    got = lax.all_to_all(sent.reshape(16, 64, 128), ("dep", "lat"), 0, 0, tiled=False)
    out = jax.ShapeDtypeStruct((FIELDS, 8, 8, 256), F32)
    return pl.pallas_call(
        finish_kernel,
        out_shape=(out, out),
        in_specs=smem(1) + vmem(1),
        out_specs=tuple(vmem(2)),
        scratch_shapes=[pltpu.VMEM((4, 256, 128), F32)],
        compiler_params=params(),
        name="finish",
    )(me, got)


def solution(mesh):
    return jax.shard_map(
        per_device,
        mesh=mesh,
        in_specs=(
            P(None, "dep", "lat", "lon"),
            P("dep", "lat", "lon"),
            P("dep", "lat", "lon"),
            P(),
            P(),
        ),
        out_specs=(P(None, "dep", "lat", "lon"), P(None, "dep", "lat", "lon")),
        check_vma=False,
    )
```
